256 devices in a mesh: ctx: 64 (over x, z, core), head: 4 (over y).
Axes of the slice: x: 4, y: 4, z: 8, core: 2. Of those that a mesh axis runs over, the one named last changes fastest.
Arguments:
- queries: bfloat16 [16384, 2048], P('ctx', 'head'), may hold values from -160 to 160
- keys: bfloat16 [16384, 512], P('ctx', 'head'), may hold values from -7 to 7
- values: bfloat16 [16384, 512], P('ctx', 'head'), may hold values from -6 to 6
- segments: int32 [16384], P('ctx'), may hold values from 0 to 2, as said below
- block_ranges: int32 [128, 3], replicated, may hold values from 0 to 127, as said below
- owner: int32 [128], replicated, may hold values from 0 to 63, as said below
- out_proj: bfloat16 [2048, 4096], P('head'), may hold values from -0.125 to 0.125
Outputs:
- attended: bfloat16 [16384, 4096], P(('ctx', 'head'))
The draws below stay inside these ranges and needn't reach their ends.
Inputs may be any that keep to these rules, and one draw needn't show every extreme that they name: `owner`: each index d of ctx owns exactly one block b with b % 2 == j for every j below 2. `block_ranges`: row b holds lo <= b <= hi and a flag of 0 or 1; hi == b where the flag is 1. `segments`: never falling along the tokens; 3 documents.
All inputs are finite; a program needn't handle non-finite values.
Results may differ from the reference program's by a relative error of at most 0.015.
Values may be sent and summed in bfloat16 or wider, within the bound.
A program may use at most 128 MiB of HBM per device.

```python
import math
import jax
import jax.numpy as jnp
from jax import lax

D = 4096
HD = 128
QH = 16
KH = 4
BLK = 128
BLK_DEV = 2
TOKENS = 16384
NBLK = 128
DOCS = 3


def base_heads(key):
    return jnp.clip(jax.random.normal(key, (TOKENS, KH, HD), jnp.float32), -6.0, 6.0)


def documents(key):
    key = jax.random.fold_in(key, 7)
    picks = jax.random.permutation(key, TOKENS - 1)[:DOCS - 1] + 1
    starts = jnp.sort(picks).astype(jnp.int32)
    positions = jnp.arange(TOKENS, dtype=jnp.int32)
    doc_ids = jnp.sum((positions[:, None] >= starts[None, :]).astype(jnp.int32), axis=1).astype(jnp.int32)
    firsts = jnp.concatenate([jnp.zeros((1,), jnp.int32), starts])
    lasts = jnp.concatenate([starts - 1, jnp.full((1,), TOKENS - 1, jnp.int32)])
    kinds = jax.random.randint(jax.random.fold_in(key, 1), (DOCS,), 0, 2).astype(jnp.int32)
    return (doc_ids, firsts, lasts, kinds)


def draw_queries(key, part):
    key = jax.random.fold_in(key, 11)
    noise = jnp.clip(jax.random.normal(key, (TOKENS, QH, HD), jnp.float32), -6.0, 6.0)
    return noise.reshape(TOKENS, QH * HD).astype(jnp.bfloat16)


def draw_keys(key, part):
    base = base_heads(key)
    return base.reshape(TOKENS, KH * HD).astype(jnp.bfloat16)


def draw_segments(key, part):
    doc_ids, firsts, lasts, kinds = documents(key)
    return doc_ids


def draw_block_ranges(key, part):
    doc_ids, firsts, lasts, kinds = documents(key)
    block_ids = jnp.arange(NBLK, dtype=jnp.int32)
    head_doc = doc_ids[block_ids * BLK]
    tail_doc = doc_ids[block_ids * BLK + BLK - 1]
    causal = 1 - kinds[tail_doc]
    low_block = firsts[head_doc] // BLK
    high_block = jnp.where(causal == 1, block_ids, lasts[tail_doc] // BLK)
    return jnp.stack([low_block, high_block, causal], axis=1).astype(jnp.int32)


def one_ordering(one_key):
    holders = NBLK // BLK_DEV
    ordering = jax.random.permutation(one_key, holders).astype(jnp.int32)
    chosen = jax.random.randint(jax.random.fold_in(one_key, 1), (), 0, holders).astype(jnp.int32)
    opposite = ((chosen + holders // 2) % holders).astype(jnp.int32)
    found_at = jnp.argmax(ordering == opposite).astype(jnp.int32)
    displaced = ordering[chosen]
    ordering = ordering.at[found_at].set(displaced)
    ordering = ordering.at[chosen].set(opposite)
    return ordering


def draw_owner(key, part):
    key = jax.random.fold_in(key, 5)
    split_keys = jax.random.split(key, BLK_DEV)
    orders = jax.vmap(one_ordering)(split_keys)
    block_ids = jnp.arange(NBLK, dtype=jnp.int32)
    return orders[block_ids % BLK_DEV, block_ids // BLK_DEV].astype(jnp.int32)


def block_scale(rng, extent, shards, low, high):
    level, own = 1.0, jax.random.fold_in(rng, 6)
    for position, shards_of in shards:
        steps = jnp.exp(jax.random.uniform(jax.random.fold_in(own, position), (shards_of,), jnp.float32, low / len(shards), high / len(shards)))
        level = level * jnp.repeat(steps, extent[position] // shards_of).reshape([-1 if axis == position else 1 for axis in range(len(extent))])
    return level


def bell_draw(key, dims, spread, reach, pieces=(), kind=jnp.bfloat16):
    values = spread * jax.random.normal(key, dims, jnp.float32)
    if pieces:
        values = values * block_scale(key, dims, pieces, -0.22, 0.18)
    return jnp.clip(values, -reach, reach).astype(kind)


def setup_inputs(seed: int = 0) -> dict:
    seeds = jax.random.split(jax.random.key(seed), 8)
    return {
        "queries": draw_queries(jax.random.fold_in(seeds[7], 71), 0),
        "keys": draw_keys(jax.random.fold_in(seeds[7], 71), 0),
        "values": bell_draw(seeds[2], (TOKENS, KH * HD), 1.0, 6.0, ((0, 64), (1, 4))),
        "segments": draw_segments(jax.random.fold_in(seeds[7], 71), 0),
        "block_ranges": draw_block_ranges(jax.random.fold_in(seeds[7], 71), 0),
        "owner": draw_owner(jax.random.fold_in(seeds[7], 71), 0),
        "out_proj": bell_draw(seeds[6], (QH * HD, D), (QH * HD) ** -0.5, 0.125, ((0, 4),)),
    }


def reference(queries, keys, values, segments, block_ranges, owner, out_proj):
    block_total = TOKENS // BLK
    group_size = QH // KH
    score_scale = 1.0 / math.sqrt(HD)
    query_blocks = queries.reshape(block_total, BLK, KH, group_size, HD)
    key_heads = keys.reshape(TOKENS, KH, HD).astype(jnp.float32)
    value_heads = values.reshape(TOKENS, KH, HD).astype(jnp.float32)
    key_pos = jnp.arange(TOKENS, dtype=jnp.int32)
    key_block = key_pos // BLK
    block_ids = jnp.arange(block_total, dtype=jnp.int32)

    def one_block(packed):
        query_block, block_index = packed
        low_block = block_ranges[block_index, 0]
        high_block = block_ranges[block_index, 1]
        causal = block_ranges[block_index, 2]
        query_pos = block_index * BLK + jnp.arange(BLK, dtype=jnp.int32)
        query_seg = lax.dynamic_slice_in_dim(segments, (block_index * BLK).astype(jnp.int32), BLK)
        visible = (key_block >= low_block)[None, :] & (key_block <= high_block)[None, :]
        visible = visible & (query_seg[:, None] == segments[None, :])
        visible = visible & ((causal == 0) | (key_pos[None, :] <= query_pos[:, None]))
        score = jnp.einsum('rgcd,kgd->gcrk', query_block.astype(jnp.float32), key_heads) * score_scale
        score = jnp.where(visible, score, -jnp.inf)
        largest = lax.optimization_barrier(jnp.max(score, axis=-1, keepdims=True))
        expo = jnp.where(visible, jnp.exp(score - largest), 0.0)
        denom = lax.optimization_barrier(jnp.sum(expo, axis=-1))
        weights = lax.optimization_barrier(expo.astype(jnp.bfloat16)).astype(jnp.float32)
        numer = jnp.einsum('gcrk,kgd->gcrd', weights, value_heads)
        result = numer / denom[..., None]
        return result.transpose(2, 0, 1, 3).reshape(BLK, QH * HD).astype(jnp.bfloat16)
    attn = lax.map(one_block, (query_blocks, block_ids))
    slot_of_block = (owner * BLK_DEV + block_ids % BLK_DEV).astype(jnp.int32)
    block_at_slot = jnp.zeros((block_total,), jnp.int32).at[slot_of_block].set(block_ids)
    owned = attn[block_at_slot].reshape(TOKENS, QH * HD)
    return jnp.dot(owned, out_proj, preferred_element_type=jnp.float32).astype(jnp.bfloat16)
```

```python
import functools
import math

import jax
import jax.numpy as jnp
from jax import lax
from jax.experimental import pallas as pl
from jax.experimental.pallas import tpu as pltpu
from jax.sharding import PartitionSpec as P

MESH = pl.DeviceIdType.MESH
HD = 128
BLK = 128
GROUP = 4
NX, NZ, CORES = 4, 8, 2
CTX = NX * NZ * CORES
HEADS = 4
ROWS = 256
KSEG = ROWS + 16
PIECE = KSEG + ROWS
DOC_STEP = 32768
MASKED = -1e30
BIAS = -(2**31)
SCALE = math.log2(math.e) / math.sqrt(HD)


def ctx_of(x, z, core):
    return (x * NZ + z) * CORES + core


def ring_offsets(size):
    half = size // 2
    found = [0]
    for step in range(1, half):
        found += [step, -step]
    return found + [half]


def piece_order(size_a, size_b):
    pieces = [(da, db) for da in ring_offsets(size_a) for db in ring_offsets(size_b)]
    return sorted(pieces, key=lambda piece: abs(piece[0]) + abs(piece[1]))


ORDERS = (piece_order(NX, NZ), piece_order(NZ, NX))


class Place:
    def __init__(self):
        ctx = lax.axis_index("ctx")
        self.ctx = ctx
        self.head = lax.axis_index("head")
        self.core = ctx % CORES
        self.z = (ctx // CORES) % NZ
        self.x = ctx // (CORES * NZ)

    def chip(self, dx, dz, core):
        return ctx_of((self.x + dx + NX) % NX, (self.z + dz + NZ) % NZ, core)

    def piece(self, role, da, db):
        dx, dz = (da, db) if role == 0 else (db, da)
        return self.chip(dx, dz, role)

    def device(self, ctx):
        return {"ctx": ctx, "head": self.head}


def gather_attend(
    queries, keys, values, segs, ranges, out,
    held, scaled, total, top, first, width, recv_sem, send_sem,
):
    place = Place()
    me = place.ctx

    barrier = pltpu.get_barrier_semaphore()
    around = [place.device(place.chip(dx, dz, place.core)) for dx, dz in ((1, 0), (-1, 0), (0, 1), (0, -1))]
    around.append(place.device(place.chip(0, 0, 1 - place.core)))
    for device in around:
        pl.semaphore_signal(barrier, inc=1, device_id=device, device_id_type=MESH)

    held[me, 0:ROWS, :] = keys[...]
    seg_rows = segs[...]
    held[me, ROWS:KSEG, :] = jnp.concatenate(
        [seg_rows.astype(jnp.float32), jnp.zeros((14, BLK), jnp.float32)], axis=0
    ).astype(jnp.bfloat16)
    held[me, KSEG:PIECE, :] = values[...]
    pl.semaphore_wait(barrier, len(around))

    parts = {"all": (0, PIECE, 0), "keys": (0, KSEG, 0), "values": (KSEG, ROWS, 1)}

    def copy(part, slot, kind, index, device):
        start, size, which = parts[part]
        rows = held.at[slot, pl.ds(start, size), :]
        return pltpu.make_async_remote_copy(
            src_ref=rows, dst_ref=rows,
            send_sem=send_sem.at[index, kind], recv_sem=recv_sem.at[slot, which],
            device_id=place.device(device), device_id_type=MESH,
        )

    def sends(role, index):
        da, db = ORDERS[role][index]
        size_a, size_b = (NX, NZ) if role == 0 else (NZ, NX)
        slot = place.piece(role, da, db)

        def along(axis, way):
            step = way if axis == 0 else 0, way if axis == 1 else 0
            dx, dz = step if role == 0 else (step[1], step[0])
            return place.chip(dx, dz, role)

        found = []

        def carry(axis, offset, size):
            if offset == 0:
                found.append(("all", slot, 2 * axis, index, along(axis, 1)))
                found.append(("all", slot, 2 * axis + 1, index, along(axis, -1)))
            elif abs(offset) < size // 2:
                way = -1 if offset > 0 else 1
                part = "all" if abs(offset) < size // 2 - 1 else ("keys" if offset > 0 else "values")
                found.append((part, slot, 2 * axis + (0 if way > 0 else 1), index, along(axis, way)))

        if db == 0:
            carry(0, da, size_a)
        carry(1, db, size_b)
        found.append(("all", slot, 4, index, place.chip(0, 0, 1 - role)))
        return found

    def arrive(role, index):
        da, db = ORDERS[role][index]
        size_a, size_b = (NX, NZ) if role == 0 else (NZ, NX)
        slot = place.piece(role, da, db)
        if da == 0 and db == 0:
            return
        halves = db == size_b // 2 or (db == 0 and da == size_a // 2)
        for part in ("keys", "values") if halves else ("all",):
            copy(part, slot, 0, index, me).wait_recv()

    def events(step):
        for role in range(2):
            for count in range(len(ORDERS[role]) // 2):

                @pl.when((place.core == role) & (step == count))
                def _(role=role, count=count):
                    for index in (2 * count, 2 * count + 1):
                        arrive(role, index)
                        for each in sends(role, index):
                            copy(*each).start()

    def slot_of(role_is, index):
        offsets = []
        for axis in range(2):
            value = jnp.int32(0)
            for role in range(2):
                for place_in in range(len(ORDERS[role])):
                    amount = ORDERS[role][place_in]
                    dx, dz = amount if role == 0 else (amount[1], amount[0])
                    value = jnp.where(
                        (role_is == role) & (index == place_in), (dx, dz)[axis], value
                    )
            offsets.append(value)
        return place.chip(offsets[0], offsets[1], role_is)

    events(jnp.int32(0))

    bounds = ranges[pl.ds(2 * me, 2), :]
    for block in range(2):
        low, high, causal = (bounds[block : block + 1, i : i + 1] for i in range(3))
        seg = jnp.transpose(
            jnp.broadcast_to(seg_rows[block : block + 1, :].astype(jnp.float32), (BLK, BLK))
        ).astype(jnp.int32)
        pos = me * ROWS + block * BLK + lax.broadcasted_iota(jnp.int32, (BLK, BLK), 0)
        start = jnp.broadcast_to(low * BLK, (BLK, BLK))
        end = jnp.broadcast_to(high * BLK + (BLK - 1), (BLK, BLK))
        end = jnp.where(jnp.broadcast_to(causal, (BLK, BLK)) == 0, end, jnp.minimum(end, pos))
        first[block * BLK : (block + 1) * BLK, :] = jnp.int32(BIAS) - (start + seg * DOC_STEP)
        width[block * BLK : (block + 1) * BLK, :] = (end - start + 1) + jnp.int32(BIAS)

    for head in range(GROUP):
        query = queries[:, head * HD : (head + 1) * HD].astype(jnp.float32) * SCALE
        large = query.astype(jnp.bfloat16)
        scaled[head, :, 0:HD] = large
        scaled[head, :, HD : 2 * HD] = (query - large.astype(jnp.float32)).astype(jnp.bfloat16)
    top[...] = jnp.full(top.shape, MASKED, jnp.float32)
    total[...] = jnp.zeros(total.shape, jnp.float32)

    def attend(slots):
        lines, key_parts, value_parts = [], [], []
        lane = lax.broadcasted_iota(jnp.int32, (1, BLK), 1)
        for slot in slots:
            key = held[slot, 0:ROWS, :]
            key_parts.append(jnp.concatenate([key, key], axis=1))
            value = held[slot, KSEG:PIECE, :]
            value_parts.append(jnp.concatenate([value, jnp.ones_like(value)], axis=1))
            docs = held[slot, ROWS:KSEG, :].astype(jnp.float32).astype(jnp.int32)
            for block in range(2):
                lines.append(docs[block : block + 1, :] * DOC_STEP + lane + (slot * ROWS + block * BLK))
        value_all = jnp.concatenate(value_parts, axis=0)
        for head in range(GROUP):
            scores = []
            for at, key in enumerate(key_parts):
                score = lax.dot_general(
                    scaled[head], key, (((1,), (1,)), ((), ())), preferred_element_type=jnp.float32
                )
                for block in range(2):
                    inside = lines[2 * at + block] + first[...] < width[...]
                    scores.append(jnp.where(inside, score[:, block * BLK : (block + 1) * BLK], MASKED))
            largest = functools.reduce(jnp.maximum, scores)
            old = top[head]
            new = jnp.maximum(old, jnp.max(largest, axis=1, keepdims=True))
            top[head] = new
            factor = jnp.exp2(old - new)
            expo = jnp.concatenate([jnp.exp2(score - new).astype(jnp.bfloat16) for score in scores], axis=1)
            added = jnp.dot(expo, value_all, preferred_element_type=jnp.float32)
            total[head, :, 0:HD] = total[head, :, 0:HD] * factor + added[:, 0:HD]
            total[head, :, HD : 2 * HD] = total[head, :, HD : 2 * HD] * factor + added[:, HD : 2 * HD]

    steps = len(ORDERS[0]) // 2

    def one_step(step, carry):
        events(step + 1)
        slots = []
        for index in range(2):
            slots.append(slot_of(place.core, 2 * step + index))
            other = slot_of(1 - place.core, 2 * step + index)
            copy("all", other, 0, 0, me).wait_recv()
            slots.append(other)
        attend(slots)
        return carry

    lax.fori_loop(0, steps, one_step, 0)

    for head in range(GROUP):
        out[:, head * HD : (head + 1) * HD] = (
            total[head, :, 0:HD] / total[head, :, HD : 2 * HD]
        ).astype(jnp.bfloat16)

    for role in range(2):

        @pl.when(place.core == role)
        def _(role=role):
            for index in range(len(ORDERS[role])):
                for each in sends(role, index):
                    copy(*each).wait_send()


def call_gather_attend(queries, keys, values, segs, ranges):
    vmem = pl.BlockSpec(memory_space=pltpu.VMEM)
    flops = 4 * GROUP * ROWS * ROWS * CTX * HD
    return pl.pallas_call(
        gather_attend,
        out_shape=jax.ShapeDtypeStruct((ROWS, GROUP * HD), jnp.bfloat16),
        in_specs=[vmem] * 5,
        out_specs=vmem,
        scratch_shapes=[
            pltpu.VMEM((CTX, PIECE, HD), jnp.bfloat16),
            pltpu.VMEM((GROUP, ROWS, 2 * HD), jnp.bfloat16),
            pltpu.VMEM((GROUP, ROWS, 2 * HD), jnp.float32),
            pltpu.VMEM((GROUP, ROWS, HD), jnp.float32),
            pltpu.VMEM((ROWS, BLK), jnp.int32),
            pltpu.VMEM((ROWS, BLK), jnp.int32),
            pltpu.SemaphoreType.DMA((CTX, 2)),
            pltpu.SemaphoreType.DMA((NX * NZ, 5)),
        ],
        compiler_params=pltpu.CompilerParams(
            collective_id=0, has_side_effects=True, vmem_limit_bytes=48 << 20
        ),
        cost_estimate=pl.CostEstimate(
            flops=flops, bytes_accessed=CTX * PIECE * HD * 2, transcendentals=GROUP * ROWS * ROWS * CTX
        ),
        name="gather_attend",
    )(queries, keys, values, segs, ranges)


def local(queries, keys, values, segments, block_ranges, owner, out_proj):
    attn = call_gather_attend(queries, keys, values, segments.reshape(2, BLK), block_ranges)
    lead = attn.reshape(2, CTX, 2, GROUP * HD).transpose(1, 0, 2, 3).reshape(CTX, 4, GROUP * HD)
    spread = lax.all_to_all(lead, "ctx", 0, 0, tiled=True).reshape(CTX, 2, 2, GROUP * HD)
    owners = owner.reshape(CTX, 2)
    home = jnp.argmax(owners[None, :, :] == jnp.arange(CTX, dtype=jnp.int32)[:, None, None], axis=1)
    moved = jnp.stack([jnp.take(spread[:, j], home[:, j], axis=0) for j in range(2)], axis=1)
    owned = lax.all_to_all(moved.reshape(CTX, 4, GROUP * HD), "ctx", 0, 0, tiled=True)
    owned = owned.reshape(CTX, 2, 2, GROUP * HD).transpose(1, 0, 2, 3).reshape(ROWS, GROUP * HD)
    product = jnp.dot(owned, out_proj, preferred_element_type=jnp.float32).astype(jnp.bfloat16)
    return lax.psum_scatter(product, "head", scatter_dimension=0, tiled=True)


def solution(mesh):
    return jax.shard_map(
        local,
        mesh=mesh,
        in_specs=(
            P("ctx", "head"),
            P("ctx", "head"),
            P("ctx", "head"),
            P("ctx"),
            P(),
            P(),
            P("head", None),
        ),
        out_specs=P(("ctx", "head"), None),
        check_vma=False,
    )
```

```python
import functools
import math

import jax
import jax.numpy as jnp
from jax import lax
from jax.experimental import pallas as pl
from jax.experimental.pallas import tpu as pltpu
from jax.sharding import PartitionSpec as P

MESH = pl.DeviceIdType.MESH
HD = 128
BLK = 128
GROUP = 4
NX, NZ, CORES = 4, 8, 2
CTX = NX * NZ * CORES
HEADS = 4
ROWS = 256
KSEG = ROWS + 16
PIECE = KSEG + ROWS
CHIPS = NX * NZ
WIDE = 4096
HALF = WIDE // 2
TURN = 32
MIXED = CHIPS * 16
CLASSES = 16
TRIPLE = 3
LOOKAHEAD = 1
DOC_STEP = 32768
MASKED = -1e30
SCALE = math.log2(math.e) / math.sqrt(HD)


def ctx_of(x, z, core):
    return (x * NZ + z) * CORES + core


def ring_offsets(size):
    half = size // 2
    found = [0]
    for step in range(1, half):
        found += [step, -step]
    return found + [half]


def piece_order(size_a, size_b):
    pieces = [(da, db) for da in ring_offsets(size_a) for db in ring_offsets(size_b)]
    return sorted(pieces, key=lambda piece: abs(piece[0]) + abs(piece[1]))


ORDERS = (piece_order(NX, NZ), piece_order(NZ, NX))


class Place:
    def __init__(self):
        ctx = lax.axis_index("ctx")
        self.ctx = ctx
        self.head = lax.axis_index("head")
        self.core = ctx % CORES
        self.z = (ctx // CORES) % NZ
        self.x = ctx // (CORES * NZ)
        self.chip_here = ctx // CORES

    def chip(self, dx, dz, core):
        return ctx_of((self.x + dx + NX) % NX, (self.z + dz + NZ) % NZ, core)

    def device(self, ctx):
        return {"ctx": ctx, "head": self.head}

    def plane(self, step):
        return (self.head + step) % HEADS


def iota(shape, dim):
    return lax.broadcasted_iota(jnp.int32, shape, dim)


def one_hot(mask):
    return jnp.where(mask, 1.0, 0.0).astype(jnp.bfloat16)


def exact(left, right):
    return jnp.dot(left, right, preferred_element_type=jnp.float32)


def kernel(
    queries_hbm, keys_hbm, values_hbm, segs_hbm, ranges_hbm, owner_hbm, proj_hbm, out,
    queries, keys, segs, ranges, owner, proj, load_sem,
    held, scaled, total, top, recv_sem, send_sem,
    attn, swap_out, swap_in, spread_out, spread_in, back_in, mix, owned, swap_send, swap_recv, spread_send, spread_recv,
    part, first_in, last_in, sum_send, sum_recv,
):
    place = Place()
    me, core, other = place.ctx, place.core, 1 - place.core

    loads = [
        pltpu.make_async_copy(source, target, load_sem.at[at])
        for at, (source, target) in enumerate(
            (
                (keys_hbm, keys),
                (segs_hbm, segs),
                (values_hbm, held.at[core, 0, pl.ds(KSEG, ROWS), :]),
                (queries_hbm, queries),
                (ranges_hbm, ranges),
                (owner_hbm, owner),
                (proj_hbm, proj),
            )
        )
    ]
    for load in loads:
        load.start()

    barrier = pltpu.get_barrier_semaphore()
    sibling = place.device(place.chip(0, 0, other))

    def greet(step, carry):
        target = place.device(place.chip(step // NZ, step % NZ, core))
        pl.semaphore_signal(barrier, inc=1, device_id=target, device_id_type=MESH)
        return carry

    lax.fori_loop(1, CHIPS, greet, 0)
    pl.semaphore_signal(barrier, inc=1, device_id=sibling, device_id_type=MESH)
    for step in (1, -1):
        pl.semaphore_signal(
            barrier, inc=1, device_id={"ctx": me, "head": place.plane(step)}, device_id_type=MESH
        )

    for load in loads[:3]:
        load.wait()
    for block in range(2):
        turned = jnp.transpose(keys[block * BLK : (block + 1) * BLK, :].astype(jnp.float32))
        held[core, 0, block * BLK : (block + 1) * BLK, :] = turned.astype(jnp.bfloat16)
    seg_rows = segs[...].astype(jnp.float32)
    held[core, 0, ROWS:KSEG, :] = jnp.concatenate(
        [seg_rows, jnp.full((1, BLK), me, jnp.int32).astype(jnp.float32), jnp.zeros((13, BLK), jnp.float32)], axis=0
    ).astype(jnp.bfloat16)
    pl.semaphore_wait(barrier, CHIPS - 1 + 1 + 2)

    parts = {"all": (0, PIECE, 0), "keys": (0, KSEG, 0), "values": (KSEG, ROWS, 1)}

    def copy(piece, name, kind, at, device):
        role, index = piece
        start, size, which = parts[name]
        return pltpu.make_async_remote_copy(
            src_ref=held.at[role, index, pl.ds(start, size), :],
            dst_ref=held.at[role, at, pl.ds(start, size), :],
            send_sem=send_sem.at[index, kind], recv_sem=recv_sem.at[role, at, which],
            device_id=place.device(device), device_id_type=MESH,
        )

    def sends(role, index):
        order = ORDERS[role]
        sizes = (NX, NZ) if role == 0 else (NZ, NX)
        offsets = order[index]
        found = []

        def go(name, axis, way):
            moved = list(offsets)
            moved[axis] -= way
            for each in range(2):
                if moved[each] <= -sizes[each] // 2:
                    moved[each] += sizes[each]
            step = [0, 0]
            step[axis] = way
            dx, dz = step if role == 0 else step[::-1]
            kind = 2 * axis + (0 if way > 0 else 1)
            found.append(copy((role, index), name, kind, order.index(tuple(moved)), place.chip(dx, dz, role)))

        for axis in range(2):
            if axis == 0 and offsets[1] != 0:
                continue
            offset, half = offsets[axis], sizes[axis] // 2
            if offset == 0:
                go("all", axis, 1)
                go("all", axis, -1)
            elif abs(offset) < half:
                name = "all" if abs(offset) < half - 1 else ("keys" if offset > 0 else "values")
                go(name, axis, -1 if offset > 0 else 1)
        found.append(copy((role, index), "all", 4, index, place.chip(0, 0, 1 - role)))
        return found

    def arrive(role, index):
        da, db = ORDERS[role][index]
        sizes = (NX, NZ) if role == 0 else (NZ, NX)
        if index == 0:
            return
        halves = db == sizes[1] // 2 or (db == 0 and da == sizes[0] // 2)
        for name in ("keys", "values") if halves else ("all",):
            copy((role, index), name, 0, index, me).wait_recv()

    def forward(indices):
        for role in range(2):

            @pl.when(core == role)
            def _(role=role):
                for index in indices:
                    arrive(role, index)
                    for each in sends(role, index):
                        each.start()

    forward((0,))

    for load in loads[3:6]:
        load.wait()
    lane = iota((1, BLK), 1)
    bounds = []
    for block in range(2):
        picked = jnp.where(lane == 2 * me + block, ranges[...], 0).astype(jnp.float32)
        bounds.append(jnp.sum(picked, axis=1, keepdims=True).astype(jnp.int32))
    row = iota((CLASSES, BLK), 0)
    low, high = (
        jnp.where(
            row < 3,
            jnp.broadcast_to(bounds[0][at : at + 1, :], (CLASSES, BLK)),
            jnp.broadcast_to(bounds[1][at : at + 1, :], (CLASSES, BLK)),
        )
        for at in range(2)
    )
    class_seg = jnp.where(row < 3, row, row - 3) * DOC_STEP
    class_from = low * BLK + class_seg
    class_to = high * BLK + (BLK - 1) + class_seg

    row_seg = [
        jnp.transpose(jnp.broadcast_to(seg_rows[block : block + 1, :], (BLK, BLK))).astype(jnp.int32)
        for block in range(2)
    ]
    row_class = jnp.concatenate([row_seg[0], row_seg[1] + 3], axis=0)
    chosen = one_hot(row_class[:, 0:CLASSES] == iota((ROWS, CLASSES), 1))
    for head in range(GROUP):
        rows = slice(head * ROWS, (head + 1) * ROWS)
        scaled[rows, 0:HD] = queries[:, head * HD : (head + 1) * HD]
        scaled[rows, HD : HD + CLASSES] = chosen

    def with_ones(value):
        return jnp.concatenate([value, jnp.ones_like(value)], axis=1)

    def line_of(role, index):
        info = held[role, index, ROWS:KSEG, :].astype(jnp.float32).astype(jnp.int32)
        base = info[2:3, :] * ROWS + lane
        return [info[block : block + 1, :] * DOC_STEP + base + block * BLK for block in range(2)]

    own_key = jnp.concatenate([held[core, 0, 0:BLK, :], held[core, 0, BLK : 2 * BLK, :]], axis=1)
    own_value = with_ones(held[core, 0, KSEG:PIECE, :])
    own_line = jnp.concatenate(line_of(core, 0), axis=1)
    inside = []
    for block in range(2):
        low, high, causal = (jnp.broadcast_to(bounds[block][i : i + 1, :], (BLK, BLK)) for i in range(3))
        pos = me * ROWS + block * BLK + iota((BLK, BLK), 0)
        end = high * BLK + (BLK - 1)
        end = jnp.where(causal == 0, end, jnp.minimum(end, pos)) + row_seg[block] * DOC_STEP
        start = low * BLK + row_seg[block] * DOC_STEP
        wide = jnp.broadcast_to(own_line, (BLK, ROWS))
        inside.append(
            (wide >= jnp.concatenate([start, start], axis=1)) & (wide <= jnp.concatenate([end, end], axis=1))
        )
    hidden = jnp.where(jnp.concatenate(inside, axis=0), 0.0, MASKED)
    for head in range(GROUP):
        rows = slice(head * ROWS, (head + 1) * ROWS)
        score = exact(scaled[rows, 0:HD], own_key)
        score = jnp.where(hidden < 0.0, MASKED, score)
        new = jnp.broadcast_to(jnp.max(score, axis=1, keepdims=True), (ROWS, HD))
        top[rows, :] = new
        expo = jnp.concatenate(
            [jnp.exp2((score[:, at * BLK : (at + 1) * BLK] - new) * SCALE).astype(jnp.bfloat16) for at in range(2)],
            axis=1,
        )
        total[rows, :] = exact(expo, own_value)

    def attend(pieces):
        key_parts, value_parts = [], []
        for role, index in pieces:
            blocks = []
            for block, line in enumerate(line_of(role, index)):
                spot = jnp.broadcast_to(line, (CLASSES, BLK))
                seen = (spot >= class_from) & (spot <= class_to)
                extra = jnp.where(seen, 0.0, MASKED).astype(jnp.bfloat16)
                blocks.append(
                    jnp.concatenate([held[role, index, block * BLK : (block + 1) * BLK, :], extra], axis=0)
                )
            key_parts.append(jnp.concatenate(blocks, axis=1))
            value_parts.append(with_ones(held[role, index, KSEG:PIECE, :]))
        value_all = jnp.concatenate(value_parts, axis=0)
        for head in range(GROUP):
            rows = slice(head * ROWS, (head + 1) * ROWS)
            scores = []
            for key in key_parts:
                score = exact(scaled[rows, 0 : HD + CLASSES], key)
                scores += [score[:, 0:BLK], score[:, BLK : 2 * BLK]]
            largest = functools.reduce(jnp.maximum, scores)
            old = top[rows, :]
            new = jnp.maximum(old, jnp.max(largest, axis=1, keepdims=True))
            top[rows, :] = new
            factor = jnp.exp2((old - new) * SCALE)
            expo = jnp.concatenate(
                [jnp.exp2((score - new) * SCALE).astype(jnp.bfloat16) for score in scores], axis=1
            )
            added = exact(expo, value_all)
            total[rows, 0:HD] = total[rows, 0:HD] * factor + added[:, 0:HD]
            total[rows, HD : 2 * HD] = total[rows, HD : 2 * HD] * factor + added[:, HD : 2 * HD]

    steps = (2 * CHIPS - 1) // TRIPLE
    reached = [0]
    for step in range(steps):
        reached.append(min(CHIPS - 1, (TRIPLE * step + 3) // 2 + LOOKAHEAD))
    reached[-1] = CHIPS - 1

    def events(step, low, high):
        if high - low == 1:
            indices = tuple(range(reached[low] + 1, reached[low + 1] + 1))
            if indices:
                forward(indices)
            return
        middle = (low + high) // 2

        @pl.when(step < middle)
        def _():
            events(step, low, middle)

        @pl.when(step >= middle)
        def _():
            events(step, middle, high)

    def one_step(step, carry):
        events(step, 0, steps)
        pieces = []
        for each in range(TRIPLE):
            at = TRIPLE * step + each
            own = at % 2
            role, index = (core + 1 + own) % 2, (at + own) // 2

            @pl.when(own == 0)
            def _(role=role, index=index):
                copy((role, index), "all", 0, index, me).wait_recv()

            pieces.append((role, index))
        attend(pieces)
        return carry

    lax.fori_loop(0, steps, one_step, 0)

    for role in range(2):

        @pl.when(core == role)
        def _(role=role):
            for index in range(CHIPS):
                for each in sends(role, index):
                    each.wait_send()

    for head in range(GROUP):
        rows = slice(head * ROWS, (head + 1) * ROWS)
        attn[head] = (total[rows, 0:HD] / total[rows, HD : 2 * HD]).astype(jnp.bfloat16)

    at_out, at_in = iota((ROWS, ROWS), 0), iota((ROWS, ROWS), 1)
    scatter_rows = one_hot(at_in == (at_out % 8) * TURN + at_out // 8)
    gather_rows = one_hot(at_in == (at_out % TURN) * 8 + ((at_out % 64) // TURN) * GROUP + at_out // 64)

    def swap(turn, way):
        return pltpu.make_async_remote_copy(
            src_ref=swap_out.at[way, turn], dst_ref=swap_in.at[way, turn],
            send_sem=swap_send.at[way, turn], recv_sem=swap_recv.at[way, turn],
            device_id=sibling, device_id_type=MESH,
        )

    def spread(turn, way):
        target = spread_in if way == 0 else back_in

        def one(step, carry):
            there = ctx_of((place.x + step // NZ) % NX, (place.z + step % NZ) % NZ, core)
            pltpu.make_async_remote_copy(
                src_ref=spread_out.at[way, turn, there // CORES], dst_ref=target.at[turn, place.chip_here],
                send_sem=spread_send.at[way, turn], recv_sem=spread_recv.at[way, turn],
                device_id=place.device(there), device_id_type=MESH,
            ).start()
            return carry

        lax.fori_loop(1, CHIPS, one, 0)
        target[turn, place.chip_here] = spread_out[way, turn, place.chip_here]

    def spread_arrived(turn, way):
        target = spread_in if way == 0 else back_in
        many = target.at[turn, pl.ds(0, CHIPS - 1)]
        pltpu.make_async_copy(many, many, spread_recv.at[way, turn]).wait()

    def spread_sent(turn, way):
        many = spread_out.at[way, turn, pl.ds(0, CHIPS - 1)]
        pltpu.make_async_copy(many, many, spread_send.at[way, turn]).wait()

    for turn in range(2):
        for block in range(2):
            planes = [
                attn[head, block * BLK + 64 * side + TURN * turn : block * BLK + 64 * side + TURN * (turn + 1), :]
                for side in range(2)
                for head in range(GROUP)
            ]
            dealt = exact(scatter_rows, jnp.concatenate(planes, axis=0)).astype(jnp.bfloat16)
            owned[turn, block] = dealt
        swap_out[0, turn] = owned[turn, other]
        swap(turn, 0).start()

    def block_core(at):
        return jnp.where((at % 16) // 8 == 0, core, other)

    came = iota((BLK, MIXED), 1)
    expand = one_hot(iota((BLK, MIXED), 0) == 2 * (2 * (came // 16) + block_core(came)) + core)
    owner_rows = jnp.broadcast_to(owner[...].astype(jnp.float32), (8, BLK)).astype(jnp.bfloat16)
    owner_of = exact(owner_rows, expand)[0:1, :].astype(jnp.int32)
    code_in = owner_of * 8 + iota((1, MIXED), 1) % 8
    leaves = iota((MIXED, BLK), 0)
    code_out = (2 * (leaves // 16) + block_core(leaves)) * 8 + leaves % 8
    for at in range(MIXED // BLK):
        columns = slice(at * BLK, (at + 1) * BLK)
        mix[:, columns] = one_hot(code_out == jnp.broadcast_to(code_in[:, columns], (MIXED, BLK)))

    def eights(rows):
        return rows.astype(jnp.float32).reshape(CHIPS, 8, HD)

    for turn in range(2):
        swap(turn, 0).wait_recv()
        both = jnp.concatenate([eights(owned[turn, core]), eights(swap_in[0, turn])], axis=1)
        spread_out[0, turn] = both.astype(jnp.bfloat16)
        spread(turn, 0)
    for turn in range(2):
        spread_arrived(turn, 0)
        came_rows = spread_in[turn].reshape(MIXED, HD)
        spread_out[1, turn] = exact(mix[...], came_rows).astype(jnp.bfloat16).reshape(CHIPS, 16, HD)
        spread(turn, 1)
    for turn in range(2):
        spread_arrived(turn, 1)
        landed = back_in[turn].astype(jnp.float32)
        owned[turn, core] = landed[:, 0:8, :].reshape(ROWS, HD).astype(jnp.bfloat16)
        swap_out[1, turn] = landed[:, 8:16, :].reshape(ROWS, HD).astype(jnp.bfloat16)
        swap(turn, 1).start()

    def give(turn, message):
        way = 1 if message % 2 == 0 else -1
        side = (0, 1, 1, 0, 0, 1)[message]
        dest = place.plane(2 if message < 2 else way)
        if message < 2:
            target = first_in.at[turn, message]
        else:
            target = last_in.at[turn, message % 2, side]
        return pltpu.make_async_remote_copy(
            src_ref=part.at[turn, dest, side], dst_ref=target,
            send_sem=sum_send.at[turn, message], recv_sem=sum_recv.at[turn, message],
            device_id={"ctx": me, "head": place.plane(way)}, device_id_type=MESH,
        )

    loads[6].wait()
    for turn in range(2):
        swap(turn, 1).wait_recv()
        owned[turn, other] = swap_in[1, turn]
        lefts = []
        for block in range(2):
            sorted_rows = exact(gather_rows, owned[turn, block]).astype(jnp.bfloat16)
            lefts.append(jnp.concatenate([sorted_rows[64 * head : 64 * (head + 1), :] for head in range(GROUP)], axis=1))
        left = jnp.concatenate(lefts, axis=0)
        for side in range(2):
            for at in range(2):
                start = side * HALF + at * (HALF // 2)
                product = exact(left, proj[:, start : start + HALF // 2]).astype(jnp.bfloat16)
                for dest in range(HEADS):
                    part[turn, dest, side, :, at * (HALF // 2) : (at + 1) * (HALF // 2)] = product[
                        dest * TURN : (dest + 1) * TURN, :
                    ]
        for message in range(4):
            give(turn, message).start()
    for turn in range(2):
        for message in (4, 5):
            way = 1 if message == 4 else -1
            side = message - 4
            give(turn, message - 4).wait_recv()
            dest = place.plane(way)
            merged = part[turn, dest, side].astype(jnp.float32) + first_in[turn, side].astype(jnp.float32)
            part[turn, dest, side] = merged.astype(jnp.bfloat16)
            give(turn, message).start()
    for turn in range(2):
        for message in range(2, 6):
            give(turn, message).wait_recv()
        for side in range(2):
            summed = part[turn, place.head, side].astype(jnp.float32)
            for way in range(2):
                summed = summed + last_in[turn, way, side].astype(jnp.float32)
            out[turn * TURN : (turn + 1) * TURN, side * HALF : (side + 1) * HALF] = summed.astype(jnp.bfloat16)

    for turn in range(2):
        for way in range(2):
            swap(turn, way).wait_send()
            spread_sent(turn, way)
        for message in range(6):
            give(turn, message).wait_send()


def local(queries, keys, values, segments, block_ranges, owner, out_proj):
    anywhere = pl.BlockSpec(memory_space=pl.ANY)
    bf16, i32, f32 = jnp.bfloat16, jnp.int32, jnp.float32
    dma = pltpu.SemaphoreType.DMA
    return pl.pallas_call(
        kernel,
        out_shape=jax.ShapeDtypeStruct((ROWS // HEADS, WIDE), bf16),
        in_specs=[anywhere] * 7,
        out_specs=pl.BlockSpec(memory_space=pltpu.VMEM),
        scratch_shapes=[
            pltpu.VMEM((ROWS, GROUP * HD), bf16),
            pltpu.VMEM((ROWS, HD), bf16),
            pltpu.VMEM((2, BLK), i32),
            pltpu.VMEM((3, 2 * CTX), i32),
            pltpu.VMEM((1, 2 * CTX), i32),
            pltpu.VMEM((GROUP * HD, WIDE), bf16),
            dma((7,)),
            pltpu.VMEM((2, CHIPS, PIECE, HD), bf16),
            pltpu.VMEM((GROUP * ROWS, 2 * HD), bf16),
            pltpu.VMEM((GROUP * ROWS, 2 * HD), f32),
            pltpu.VMEM((GROUP * ROWS, HD), f32),
            dma((2, CHIPS, 2)),
            dma((CHIPS, 5)),
            pltpu.VMEM((GROUP, ROWS, HD), bf16),
            pltpu.VMEM((2, 2, ROWS, HD), bf16),
            pltpu.VMEM((2, 2, ROWS, HD), bf16),
            pltpu.VMEM((2, 2, CHIPS, 16, HD), bf16),
            pltpu.VMEM((2, CHIPS, 16, HD), bf16),
            pltpu.VMEM((2, CHIPS, 16, HD), bf16),
            pltpu.VMEM((MIXED, MIXED), bf16),
            pltpu.VMEM((2, 2, ROWS, HD), bf16),
            dma((2, 2)),
            dma((2, 2)),
            dma((2, 2)),
            dma((2, 2)),
            pltpu.VMEM((2, HEADS, 2, TURN, HALF), bf16),
            pltpu.VMEM((2, 2, TURN, HALF), bf16),
            pltpu.VMEM((2, 2, 2, TURN, HALF), bf16),
            dma((2, 6)),
            dma((2, 6)),
        ],
        compiler_params=pltpu.CompilerParams(
            collective_id=0, has_side_effects=True, vmem_limit_bytes=48 << 20
        ),
        cost_estimate=pl.CostEstimate(
            flops=4 * GROUP * ROWS * ROWS * CTX * HD,
            bytes_accessed=GROUP * HD * WIDE * 2,
            transcendentals=GROUP * ROWS * ROWS * CTX,
        ),
        name="attend_and_project",
    )(
        queries, keys, values, segments.reshape(2, BLK), block_ranges.T, owner.reshape(1, 2 * CTX), out_proj
    )


def solution(mesh):
    return jax.shard_map(
        local,
        mesh=mesh,
        in_specs=(
            P("ctx", "head"),
            P("ctx", "head"),
            P("ctx", "head"),
            P("ctx"),
            P(),
            P(),
            P("head", None),
        ),
        out_specs=P(("ctx", "head"), None),
        check_vma=False,
    )
```

```python
import functools
import math

import jax
import jax.numpy as jnp
from jax import lax
from jax.experimental import pallas as pl
from jax.experimental.pallas import tpu as pltpu
from jax.sharding import PartitionSpec as P

MESH = pl.DeviceIdType.MESH
HD = 128
BLK = 128
GROUP = 4
NX, NZ, CORES = 4, 8, 2
CTX = NX * NZ * CORES
HEADS = 4
ROWS = 256
KSEG = ROWS + 16
PIECE = KSEG + ROWS
CHIPS = NX * NZ
WIDE = 4096
HALF = WIDE // 2
TURN = 32
MIXED = CHIPS * 16
CLASSES = 16
BATCH = 4
LOOKAHEAD = 3
DOC_STEP = 32768
MASKED = -1e30
SCALE = math.log2(math.e) / math.sqrt(HD)


def ctx_of(x, z, core):
    return (x * NZ + z) * CORES + core


def ring_offsets(size):
    half = size // 2
    found = [0]
    for step in range(1, half):
        found += [step, -step]
    return found + [half]


def piece_order(size_a, size_b):
    pieces = [(da, db) for da in ring_offsets(size_a) for db in ring_offsets(size_b)]
    return sorted(pieces, key=lambda piece: abs(piece[0]) + abs(piece[1]))


ORDERS = (piece_order(NX, NZ), piece_order(NZ, NX))


class Place:
    def __init__(self):
        ctx = lax.axis_index("ctx")
        self.ctx = ctx
        self.head = lax.axis_index("head")
        self.core = ctx % CORES
        self.z = (ctx // CORES) % NZ
        self.x = ctx // (CORES * NZ)
        self.chip_here = ctx // CORES

    def chip(self, dx, dz, core):
        return ctx_of((self.x + dx + NX) % NX, (self.z + dz + NZ) % NZ, core)

    def device(self, ctx):
        return {"ctx": ctx, "head": self.head}

    def plane(self, step):
        return (self.head + step) % HEADS


def iota(shape, dim):
    return lax.broadcasted_iota(jnp.int32, shape, dim)


def one_hot(mask):
    return jnp.where(mask, 1.0, 0.0).astype(jnp.bfloat16)


def exact(left, right):
    return jnp.dot(left, right, preferred_element_type=jnp.float32)


def kernel(
    queries_hbm, keys_hbm, values_hbm, segs_hbm, ranges_hbm, owner_hbm, proj_hbm, out,
    queries, keys, segs, ranges, owner, proj, load_sem,
    held, scaled, total, top, recv_sem, send_sem,
    attn, swap_out, swap_in, spread_out, spread_in, back_in, mix, owned, swap_send, swap_recv, spread_send, spread_recv,
    part, first_in, last_in, sum_send, sum_recv,
):
    place = Place()
    me, core, other = place.ctx, place.core, 1 - place.core

    loads = [
        pltpu.make_async_copy(source, target, load_sem.at[at])
        for at, (source, target) in enumerate(
            (
                (keys_hbm, keys),
                (segs_hbm, segs),
                (values_hbm, held.at[core, 0, pl.ds(KSEG, ROWS), :]),
                (queries_hbm, queries),
                (ranges_hbm, ranges),
                (owner_hbm, owner),
                (proj_hbm, proj),
            )
        )
    ]
    for load in loads:
        load.start()

    barrier = pltpu.get_barrier_semaphore()
    sibling = place.device(place.chip(0, 0, other))

    around = [place.device(place.chip(dx, dz, core)) for dx, dz in ((1, 0), (-1, 0), (0, 1), (0, -1))]
    around += [sibling] + [{"ctx": me, "head": place.plane(step)} for step in (1, -1)]
    for device in around:
        pl.semaphore_signal(barrier, inc=1, device_id=device, device_id_type=MESH)

    for load in loads[:3]:
        load.wait()
    for block in range(2):
        turned = jnp.transpose(keys[block * BLK : (block + 1) * BLK, :].astype(jnp.float32))
        held[core, 0, block * BLK : (block + 1) * BLK, :] = turned.astype(jnp.bfloat16)
    seg_rows = segs[...].astype(jnp.float32)
    held[core, 0, ROWS:KSEG, :] = jnp.concatenate(
        [seg_rows, jnp.full((1, BLK), me, jnp.int32).astype(jnp.float32), jnp.zeros((13, BLK), jnp.float32)], axis=0
    ).astype(jnp.bfloat16)
    pl.semaphore_wait(barrier, len(around))

    parts = {"all": (0, PIECE, 0), "keys": (0, KSEG, 0), "values": (KSEG, ROWS, 1)}

    def copy(piece, name, kind, at, device):
        role, index = piece
        start, size, which = parts[name]
        return pltpu.make_async_remote_copy(
            src_ref=held.at[role, index, pl.ds(start, size), :],
            dst_ref=held.at[role, at, pl.ds(start, size), :],
            send_sem=send_sem.at[index, kind], recv_sem=recv_sem.at[role, at, which],
            device_id=place.device(device), device_id_type=MESH,
        )

    def sends(role, index):
        order = ORDERS[role]
        sizes = (NX, NZ) if role == 0 else (NZ, NX)
        offsets = order[index]
        found = []

        def go(name, axis, way):
            moved = list(offsets)
            moved[axis] -= way
            for each in range(2):
                if moved[each] <= -sizes[each] // 2:
                    moved[each] += sizes[each]
            step = [0, 0]
            step[axis] = way
            dx, dz = step if role == 0 else step[::-1]
            kind = 2 * axis + (0 if way > 0 else 1)
            found.append(copy((role, index), name, kind, order.index(tuple(moved)), place.chip(dx, dz, role)))

        for axis in range(2):
            if axis == 0 and offsets[1] != 0:
                continue
            offset, half = offsets[axis], sizes[axis] // 2
            if offset == 0:
                go("all", axis, 1)
                go("all", axis, -1)
            elif abs(offset) < half:
                name = "all" if abs(offset) < half - 1 else ("keys" if offset > 0 else "values")
                go(name, axis, -1 if offset > 0 else 1)
        found.append(copy((role, index), "all", 4, index, place.chip(0, 0, 1 - role)))
        return found

    def arrive(role, index):
        da, db = ORDERS[role][index]
        sizes = (NX, NZ) if role == 0 else (NZ, NX)
        if index == 0:
            return
        halves = db == sizes[1] // 2 or (db == 0 and da == sizes[0] // 2)
        for name in ("keys", "values") if halves else ("all",):
            copy((role, index), name, 0, index, me).wait_recv()

    def forward(indices):
        for role in range(2):

            @pl.when(core == role)
            def _(role=role):
                for index in indices:
                    arrive(role, index)
                    for each in sends(role, index):
                        each.start()

    forward((0,))

    for load in loads[3:6]:
        load.wait()
    lane = iota((1, BLK), 1)
    bounds = []
    for block in range(2):
        picked = jnp.where(lane == 2 * me + block, ranges[...], 0).astype(jnp.float32)
        bounds.append(jnp.sum(picked, axis=1, keepdims=True).astype(jnp.int32))
    row = iota((CLASSES, BLK), 0)
    low, high = (
        jnp.where(
            row < 3,
            jnp.broadcast_to(bounds[0][at : at + 1, :], (CLASSES, BLK)),
            jnp.broadcast_to(bounds[1][at : at + 1, :], (CLASSES, BLK)),
        )
        for at in range(2)
    )
    class_seg = jnp.where(row < 3, row, row - 3) * DOC_STEP
    class_from = low * BLK + class_seg
    class_to = high * BLK + (BLK - 1) + class_seg

    row_seg = [
        jnp.transpose(jnp.broadcast_to(seg_rows[block : block + 1, :], (BLK, BLK))).astype(jnp.int32)
        for block in range(2)
    ]
    row_class = jnp.concatenate([row_seg[0], row_seg[1] + 3], axis=0)
    chosen = one_hot(row_class[:, 0:CLASSES] == iota((ROWS, CLASSES), 1))
    for head in range(GROUP):
        rows = slice(head * ROWS, (head + 1) * ROWS)
        scaled[rows, 0:HD] = queries[:, head * HD : (head + 1) * HD]
        scaled[rows, HD : HD + CLASSES] = chosen

    def with_ones(value):
        return jnp.concatenate([value, jnp.ones_like(value)], axis=1)

    def line_of(role, index):
        info = held[role, index, ROWS:KSEG, :].astype(jnp.float32).astype(jnp.int32)
        base = info[2:3, :] * ROWS + lane
        return [info[block : block + 1, :] * DOC_STEP + base + block * BLK for block in range(2)]

    own_key = jnp.concatenate([held[core, 0, 0:BLK, :], held[core, 0, BLK : 2 * BLK, :]], axis=1)
    own_value = with_ones(held[core, 0, KSEG:PIECE, :])
    own_line = jnp.concatenate(line_of(core, 0), axis=1)
    inside = []
    for block in range(2):
        low, high, causal = (jnp.broadcast_to(bounds[block][i : i + 1, :], (BLK, BLK)) for i in range(3))
        pos = me * ROWS + block * BLK + iota((BLK, BLK), 0)
        end = high * BLK + (BLK - 1)
        end = jnp.where(causal == 0, end, jnp.minimum(end, pos)) + row_seg[block] * DOC_STEP
        start = low * BLK + row_seg[block] * DOC_STEP
        wide = jnp.broadcast_to(own_line, (BLK, ROWS))
        inside.append(
            (wide >= jnp.concatenate([start, start], axis=1)) & (wide <= jnp.concatenate([end, end], axis=1))
        )
    hidden = jnp.where(jnp.concatenate(inside, axis=0), 0.0, MASKED)
    for head in range(GROUP):
        rows = slice(head * ROWS, (head + 1) * ROWS)
        score = exact(scaled[rows, 0:HD], own_key)
        score = jnp.where(hidden < 0.0, MASKED, score)
        new = jnp.broadcast_to(jnp.max(score, axis=1, keepdims=True), (ROWS, HD))
        top[rows, :] = new
        expo = jnp.concatenate(
            [jnp.exp2((score[:, at * BLK : (at + 1) * BLK] - new) * SCALE).astype(jnp.bfloat16) for at in range(2)],
            axis=1,
        )
        total[rows, :] = exact(expo, own_value)

    def attend(pieces):
        key_parts, value_parts = [], []
        for role, index in pieces:
            blocks = []
            for block, line in enumerate(line_of(role, index)):
                spot = jnp.broadcast_to(line, (CLASSES, BLK))
                seen = (spot >= class_from) & (spot <= class_to)
                extra = jnp.where(seen, 0.0, MASKED).astype(jnp.bfloat16)
                blocks.append(
                    jnp.concatenate([held[role, index, block * BLK : (block + 1) * BLK, :], extra], axis=0)
                )
            key_parts.append(jnp.concatenate(blocks, axis=1))
            value_parts.append(with_ones(held[role, index, KSEG:PIECE, :]))
        value_all = jnp.concatenate(value_parts, axis=0)
        by_head = []
        for head in range(GROUP):
            rows = slice(head * ROWS, (head + 1) * ROWS)
            scores = []
            for key in key_parts:
                score = exact(scaled[rows, 0 : HD + CLASSES], key)
                scores += [score[:, 0:BLK], score[:, BLK : 2 * BLK]]
            by_head.append(scores)
        for head in range(GROUP):
            rows = slice(head * ROWS, (head + 1) * ROWS)
            scores = by_head[head]
            largest = functools.reduce(jnp.maximum, scores)
            old = top[rows, :]
            new = jnp.maximum(old, jnp.max(largest, axis=1, keepdims=True))
            top[rows, :] = new
            factor = jnp.exp2((old - new) * SCALE)
            expo = jnp.concatenate(
                [jnp.exp2((score - new) * SCALE).astype(jnp.bfloat16) for score in scores], axis=1
            )
            added = exact(expo, value_all)
            total[rows, 0:HD] = total[rows, 0:HD] * factor + added[:, 0:HD]
            total[rows, HD : 2 * HD] = total[rows, HD : 2 * HD] * factor + added[:, HD : 2 * HD]

    start = (2 * CHIPS - 1) % BATCH
    steps = (2 * CHIPS - 1) // BATCH
    reached = [min(CHIPS - 1, (start + BATCH * step) // 2 + LOOKAHEAD) for step in range(steps)] + [CHIPS - 1]

    def events(step, low, high):
        if high - low == 1:
            indices = tuple(range(reached[low] + 1, reached[low + 1] + 1))
            if indices:
                forward(indices)
            return
        middle = (low + high) // 2

        @pl.when(step < middle)
        def _():
            events(step, low, middle)

        @pl.when(step >= middle)
        def _():
            events(step, middle, high)

    def take(at):
        own = at % 2
        role, index = (core + 1 + own) % 2, (at + own) // 2

        @pl.when(own == 0)
        def _():
            copy((role, index), "all", 0, index, me).wait_recv()

        return role, index

    forward(tuple(range(1, reached[0] + 1)))
    attend([take(jnp.int32(at)) for at in range(start)])

    def one_step(step, carry):
        events(step, 0, steps)
        attend([take(start + BATCH * step + each) for each in range(BATCH)])
        return carry

    lax.fori_loop(0, steps, one_step, 0)

    for role in range(2):

        @pl.when(core == role)
        def _(role=role):
            for index in range(CHIPS):
                for each in sends(role, index):
                    each.wait_send()

    for head in range(GROUP):
        rows = slice(head * ROWS, (head + 1) * ROWS)
        attn[head] = (total[rows, 0:HD] / total[rows, HD : 2 * HD]).astype(jnp.bfloat16)

    at_out, at_in = iota((ROWS, ROWS), 0), iota((ROWS, ROWS), 1)
    scatter_rows = one_hot(at_in == (at_out % 8) * TURN + at_out // 8)
    gather_rows = one_hot(at_in == (at_out % TURN) * 8 + ((at_out % 64) // TURN) * GROUP + at_out // 64)

    def swap(turn, way):
        return pltpu.make_async_remote_copy(
            src_ref=swap_out.at[way, turn], dst_ref=swap_in.at[way, turn],
            send_sem=swap_send.at[way, turn], recv_sem=swap_recv.at[way, turn],
            device_id=sibling, device_id_type=MESH,
        )

    def spread(turn, way):
        target = spread_in if way == 0 else back_in

        def one(step, carry):
            there = ctx_of((place.x + step // NZ) % NX, (place.z + step % NZ) % NZ, core)
            pltpu.make_async_remote_copy(
                src_ref=spread_out.at[way, turn, there // CORES], dst_ref=target.at[turn, place.chip_here],
                send_sem=spread_send.at[way, turn], recv_sem=spread_recv.at[way, turn],
                device_id=place.device(there), device_id_type=MESH,
            ).start()
            return carry

        lax.fori_loop(1, CHIPS, one, 0)
        target[turn, place.chip_here] = spread_out[way, turn, place.chip_here]

    def spread_arrived(turn, way):
        target = spread_in if way == 0 else back_in
        many = target.at[turn, pl.ds(0, CHIPS - 1)]
        pltpu.make_async_copy(many, many, spread_recv.at[way, turn]).wait()

    def spread_sent(turn, way):
        many = spread_out.at[way, turn, pl.ds(0, CHIPS - 1)]
        pltpu.make_async_copy(many, many, spread_send.at[way, turn]).wait()

    for turn in range(2):
        for block in range(2):
            planes = [
                attn[head, block * BLK + 64 * side + TURN * turn : block * BLK + 64 * side + TURN * (turn + 1), :]
                for side in range(2)
                for head in range(GROUP)
            ]
            dealt = exact(scatter_rows, jnp.concatenate(planes, axis=0)).astype(jnp.bfloat16)
            owned[turn, block] = dealt
        swap_out[0, turn] = owned[turn, other]
        swap(turn, 0).start()

    def block_core(at):
        return jnp.where((at % 16) // 8 == 0, core, other)

    came = iota((BLK, MIXED), 1)
    expand = one_hot(iota((BLK, MIXED), 0) == 2 * (2 * (came // 16) + block_core(came)) + core)
    owner_rows = jnp.broadcast_to(owner[...].astype(jnp.float32), (8, BLK)).astype(jnp.bfloat16)
    owner_of = exact(owner_rows, expand)[0:1, :].astype(jnp.int32)
    code_in = owner_of * 8 + iota((1, MIXED), 1) % 8
    leaves = iota((MIXED, BLK), 0)
    code_out = (2 * (leaves // 16) + block_core(leaves)) * 8 + leaves % 8
    for at in range(MIXED // BLK):
        columns = slice(at * BLK, (at + 1) * BLK)
        mix[:, columns] = one_hot(code_out == jnp.broadcast_to(code_in[:, columns], (MIXED, BLK)))

    def eights(rows):
        return rows.astype(jnp.float32).reshape(CHIPS, 8, HD)

    def deal(turn):
        swap(turn, 0).wait_recv()
        both = jnp.concatenate([eights(owned[turn, core]), eights(swap_in[0, turn])], axis=1)
        spread_out[0, turn] = both.astype(jnp.bfloat16)
        spread(turn, 0)

    def reorder(turn):
        spread_arrived(turn, 0)
        came_rows = spread_in[turn].reshape(MIXED, HD)
        spread_out[1, turn] = exact(mix[...], came_rows).astype(jnp.bfloat16).reshape(CHIPS, 16, HD)
        spread(turn, 1)

    def collect(turn):
        spread_arrived(turn, 1)
        landed = back_in[turn].astype(jnp.float32)
        owned[turn, core] = landed[:, 0:8, :].reshape(ROWS, HD).astype(jnp.bfloat16)
        swap_out[1, turn] = landed[:, 8:16, :].reshape(ROWS, HD).astype(jnp.bfloat16)
        swap(turn, 1).start()

    def give(turn, message):
        way = 1 if message % 2 == 0 else -1
        side = (0, 1, 1, 0, 0, 1)[message]
        dest = place.plane(2 if message < 2 else way)
        if message < 2:
            target = first_in.at[turn, message]
        else:
            target = last_in.at[turn, message % 2, side]
        return pltpu.make_async_remote_copy(
            src_ref=part.at[turn, dest, side], dst_ref=target,
            send_sem=sum_send.at[turn, message], recv_sem=sum_recv.at[turn, message],
            device_id={"ctx": me, "head": place.plane(way)}, device_id_type=MESH,
        )

    def project(turn):
        swap(turn, 1).wait_recv()
        owned[turn, other] = swap_in[1, turn]
        lefts = []
        for block in range(2):
            sorted_rows = exact(gather_rows, owned[turn, block]).astype(jnp.bfloat16)
            lefts.append(jnp.concatenate([sorted_rows[64 * head : 64 * (head + 1), :] for head in range(GROUP)], axis=1))
        left = jnp.concatenate(lefts, axis=0)
        for side in range(2):
            for at in range(2):
                start = side * HALF + at * (HALF // 2)
                product = exact(left, proj[:, start : start + HALF // 2]).astype(jnp.bfloat16)
                for dest in range(HEADS):
                    part[turn, dest, side, :, at * (HALF // 2) : (at + 1) * (HALF // 2)] = product[
                        dest * TURN : (dest + 1) * TURN, :
                    ]
        for message in range(4):
            give(turn, message).start()
    def relay(turn):
        for message in (4, 5):
            way = 1 if message == 4 else -1
            side = message - 4
            give(turn, message - 4).wait_recv()
            dest = place.plane(way)
            merged = part[turn, dest, side].astype(jnp.float32) + first_in[turn, side].astype(jnp.float32)
            part[turn, dest, side] = merged.astype(jnp.bfloat16)
            give(turn, message).start()

    def finish(turn):
        for message in range(2, 6):
            give(turn, message).wait_recv()
        for side in range(2):
            summed = part[turn, place.head, side].astype(jnp.float32)
            for way in range(2):
                summed = summed + last_in[turn, way, side].astype(jnp.float32)
            out[turn * TURN : (turn + 1) * TURN, side * HALF : (side + 1) * HALF] = summed.astype(jnp.bfloat16)

    deal(0)
    deal(1)
    loads[6].wait()
    reorder(0)
    collect(0)
    project(0)
    reorder(1)
    relay(0)
    collect(1)
    project(1)
    relay(1)
    finish(0)
    finish(1)

    for turn in range(2):
        for way in range(2):
            swap(turn, way).wait_send()
            spread_sent(turn, way)
        for message in range(6):
            give(turn, message).wait_send()


def local(queries, keys, values, segments, block_ranges, owner, out_proj):
    anywhere = pl.BlockSpec(memory_space=pltpu.HBM)
    bf16, i32, f32 = jnp.bfloat16, jnp.int32, jnp.float32
    dma = pltpu.SemaphoreType.DMA
    return pl.pallas_call(
        kernel,
        out_shape=jax.ShapeDtypeStruct((ROWS // HEADS, WIDE), bf16),
        in_specs=[anywhere] * 7,
        out_specs=pl.BlockSpec(memory_space=pltpu.VMEM),
        scratch_shapes=[
            pltpu.VMEM((ROWS, GROUP * HD), bf16),
            pltpu.VMEM((ROWS, HD), bf16),
            pltpu.VMEM((2, BLK), i32),
            pltpu.VMEM((3, 2 * CTX), i32),
            pltpu.VMEM((1, 2 * CTX), i32),
            pltpu.VMEM((GROUP * HD, WIDE), bf16),
            dma((7,)),
            pltpu.VMEM((2, CHIPS, PIECE, HD), bf16),
            pltpu.VMEM((GROUP * ROWS, 2 * HD), bf16),
            pltpu.VMEM((GROUP * ROWS, 2 * HD), f32),
            pltpu.VMEM((GROUP * ROWS, HD), f32),
            dma((2, CHIPS, 2)),
            dma((CHIPS, 5)),
            pltpu.VMEM((GROUP, ROWS, HD), bf16),
            pltpu.VMEM((2, 2, ROWS, HD), bf16),
            pltpu.VMEM((2, 2, ROWS, HD), bf16),
            pltpu.VMEM((2, 2, CHIPS, 16, HD), bf16),
            pltpu.VMEM((2, CHIPS, 16, HD), bf16),
            pltpu.VMEM((2, CHIPS, 16, HD), bf16),
            pltpu.VMEM((MIXED, MIXED), bf16),
            pltpu.VMEM((2, 2, ROWS, HD), bf16),
            dma((2, 2)),
            dma((2, 2)),
            dma((2, 2)),
            dma((2, 2)),
            pltpu.VMEM((2, HEADS, 2, TURN, HALF), bf16),
            pltpu.VMEM((2, 2, TURN, HALF), bf16),
            pltpu.VMEM((2, 2, 2, TURN, HALF), bf16),
            dma((2, 6)),
            dma((2, 6)),
        ],
        compiler_params=pltpu.CompilerParams(
            collective_id=0, has_side_effects=True, vmem_limit_bytes=60 << 20
        ),
        cost_estimate=pl.CostEstimate(
            flops=4 * GROUP * ROWS * ROWS * CTX * HD,
            bytes_accessed=GROUP * HD * WIDE * 2,
            transcendentals=GROUP * ROWS * ROWS * CTX,
        ),
        name="attend_and_project",
    )(
        queries, keys, values, segments.reshape(2, BLK), block_ranges.T, owner.reshape(1, 2 * CTX), out_proj
    )


def solution(mesh):
    return jax.shard_map(
        local,
        mesh=mesh,
        in_specs=(
            P("ctx", "head"),
            P("ctx", "head"),
            P("ctx", "head"),
            P("ctx"),
            P(),
            P(),
            P("head", None),
        ),
        out_specs=P(("ctx", "head"), None),
        check_vma=False,
    )
```

```python
import functools
import math

import jax
import jax.numpy as jnp
from jax import lax
from jax.experimental import pallas as pl
from jax.experimental.pallas import tpu as pltpu
from jax.sharding import PartitionSpec as P

MESH = pl.DeviceIdType.MESH
HD = 128
BLK = 128
GROUP = 4
NX, NZ, CORES = 4, 8, 2
CTX = NX * NZ * CORES
HEADS = 4
ROWS = 256
KSEG = ROWS + 16
PIECE = KSEG + ROWS
CHIPS = NX * NZ
WIDE = 4096
HALF = WIDE // 2
TURN = 32
MIXED = CHIPS * 16
CLASSES = 16
BATCH = 4
LOOKAHEAD = 3
LAG = 5
DOC_STEP = 32768
MASKED = -1e30
SCALE = math.log2(math.e) / math.sqrt(HD)


def ctx_of(x, z, core):
    return (x * NZ + z) * CORES + core


def ring_offsets(size):
    half = size // 2
    found = [0]
    for step in range(1, half):
        found += [step, -step]
    return found + [half]


def piece_order(size_a, size_b):
    pieces = [(da, db) for da in ring_offsets(size_a) for db in ring_offsets(size_b)]
    return sorted(pieces, key=lambda piece: abs(piece[0]) + abs(piece[1]))


ORDERS = (piece_order(NX, NZ), piece_order(NZ, NX))


class Place:
    def __init__(self):
        ctx = lax.axis_index("ctx")
        self.ctx = ctx
        self.head = lax.axis_index("head")
        self.core = ctx % CORES
        self.z = (ctx // CORES) % NZ
        self.x = ctx // (CORES * NZ)
        self.chip_here = ctx // CORES

    def chip(self, dx, dz, core):
        return ctx_of((self.x + dx + NX) % NX, (self.z + dz + NZ) % NZ, core)

    def device(self, ctx):
        return {"ctx": ctx, "head": self.head}

    def plane(self, step):
        return (self.head + step) % HEADS


def iota(shape, dim):
    return lax.broadcasted_iota(jnp.int32, shape, dim)


def one_hot(mask):
    return jnp.where(mask, 1.0, 0.0).astype(jnp.bfloat16)


def exact(left, right):
    return jnp.dot(left, right, preferred_element_type=jnp.float32)


def kernel(
    queries_hbm, keys_hbm, values_hbm, segs_hbm, ranges_hbm, owner_hbm, proj_hbm, out,
    queries, keys, segs, ranges, owner, proj, load_sem,
    held, scaled, total, top, recv_sem, send_sem,
    shuffle, swap_out, swap_in, spread_out, spread_in, back_in, mix, owned, swap_send, swap_recv, spread_send, spread_recv,
    part, first_in, last_in, sum_send, sum_recv,
):
    place = Place()
    me, core, other = place.ctx, place.core, 1 - place.core

    loads = [
        pltpu.make_async_copy(source, target, load_sem.at[at])
        for at, (source, target) in enumerate(
            (
                (keys_hbm, keys),
                (segs_hbm, segs),
                (values_hbm, held.at[core, 0, pl.ds(KSEG, ROWS), :]),
                (queries_hbm, queries),
                (ranges_hbm, ranges),
                (owner_hbm, owner),
                (proj_hbm, proj),
            )
        )
    ]
    for load in loads:
        load.start()

    barrier = pltpu.get_barrier_semaphore()
    sibling = place.device(place.chip(0, 0, other))

    around = [place.device(place.chip(dx, dz, core)) for dx, dz in ((1, 0), (-1, 0), (0, 1), (0, -1))]
    around += [sibling] + [{"ctx": me, "head": place.plane(step)} for step in (1, -1)]
    for device in around:
        pl.semaphore_signal(barrier, inc=1, device_id=device, device_id_type=MESH)

    for load in loads[:3]:
        load.wait()
    for block in range(2):
        turned = jnp.transpose(keys[block * BLK : (block + 1) * BLK, :].astype(jnp.float32))
        held[core, 0, block * BLK : (block + 1) * BLK, :] = turned.astype(jnp.bfloat16)
    seg_rows = segs[...].astype(jnp.float32)
    held[core, 0, ROWS:KSEG, :] = jnp.concatenate(
        [seg_rows, jnp.full((1, BLK), me, jnp.int32).astype(jnp.float32), jnp.zeros((13, BLK), jnp.float32)], axis=0
    ).astype(jnp.bfloat16)
    pl.semaphore_wait(barrier, len(around))

    parts = {"all": (0, PIECE, 0), "keys": (0, KSEG, 0), "values": (KSEG, ROWS, 1)}

    def copy(piece, name, kind, at, device):
        role, index = piece
        start, size, which = parts[name]
        return pltpu.make_async_remote_copy(
            src_ref=held.at[role, index, pl.ds(start, size), :],
            dst_ref=held.at[role, at, pl.ds(start, size), :],
            send_sem=send_sem.at[index, kind], recv_sem=recv_sem.at[role, at, which],
            device_id=place.device(device), device_id_type=MESH,
        )

    def sends(role, index):
        order = ORDERS[role]
        sizes = (NX, NZ) if role == 0 else (NZ, NX)
        offsets = order[index]
        found = []

        def go(name, axis, way):
            moved = list(offsets)
            moved[axis] -= way
            for each in range(2):
                if moved[each] <= -sizes[each] // 2:
                    moved[each] += sizes[each]
            step = [0, 0]
            step[axis] = way
            dx, dz = step if role == 0 else step[::-1]
            kind = 2 * axis + (0 if way > 0 else 1)
            found.append(copy((role, index), name, kind, order.index(tuple(moved)), place.chip(dx, dz, role)))

        for axis in range(2):
            if axis == 0 and offsets[1] != 0:
                continue
            offset, half = offsets[axis], sizes[axis] // 2
            if offset == 0:
                go("all", axis, 1)
                go("all", axis, -1)
            elif abs(offset) < half:
                name = "all" if abs(offset) < half - 1 else ("keys" if offset > 0 else "values")
                go(name, axis, -1 if offset > 0 else 1)
        found.append(copy((role, index), "all", 4, index, place.chip(0, 0, 1 - role)))
        return found

    def arrive(role, index):
        da, db = ORDERS[role][index]
        sizes = (NX, NZ) if role == 0 else (NZ, NX)
        if index == 0:
            return
        halves = db == sizes[1] // 2 or (db == 0 and da == sizes[0] // 2)
        for name in ("keys", "values") if halves else ("all",):
            copy((role, index), name, 0, index, me).wait_recv()

    def forward(indices):
        for role in range(2):

            @pl.when(core == role)
            def _(role=role):
                for index in indices:
                    arrive(role, index)
                    for each in sends(role, index):
                        each.start()

    forward((0,))

    for load in loads[3:6]:
        load.wait()
    lane = iota((1, BLK), 1)
    bounds = []
    for block in range(2):
        picked = jnp.where(lane == 2 * me + block, ranges[...], 0).astype(jnp.float32)
        bounds.append(jnp.sum(picked, axis=1, keepdims=True).astype(jnp.int32))
    row = iota((CLASSES, BLK), 0)
    low, high = (
        jnp.where(
            row < 3,
            jnp.broadcast_to(bounds[0][at : at + 1, :], (CLASSES, BLK)),
            jnp.broadcast_to(bounds[1][at : at + 1, :], (CLASSES, BLK)),
        )
        for at in range(2)
    )
    class_seg = jnp.where(row < 3, row, row - 3) * DOC_STEP
    class_from = low * BLK + class_seg
    class_to = high * BLK + (BLK - 1) + class_seg

    row_seg = [
        jnp.transpose(jnp.broadcast_to(seg_rows[block : block + 1, :], (BLK, BLK))).astype(jnp.int32)
        for block in range(2)
    ]
    row_class = jnp.concatenate([row_seg[0], row_seg[1] + 3], axis=0)
    chosen = one_hot(row_class[:, 0:CLASSES] == iota((ROWS, CLASSES), 1))
    def by_turn(array, turn):
        starts = [block * BLK + side * 2 * TURN + turn * TURN for block in range(2) for side in range(2)]
        return jnp.concatenate([array[start : start + TURN, :] for start in starts], axis=0)

    def rows_of(turn, head):
        start = turn * GROUP * BLK + head * BLK
        return slice(start, start + BLK)

    all_queries = queries[...]
    for turn in range(2):
        turn_queries, turn_chosen = by_turn(all_queries, turn), by_turn(chosen, turn)
        for head in range(GROUP):
            scaled[rows_of(turn, head), 0:HD] = turn_queries[:, head * HD : (head + 1) * HD]
            scaled[rows_of(turn, head), HD : HD + CLASSES] = turn_chosen

    def with_ones(value):
        return jnp.concatenate([value, jnp.ones_like(value)], axis=1)

    def line_of(role, index):
        info = held[role, index, ROWS:KSEG, :].astype(jnp.float32).astype(jnp.int32)
        base = info[2:3, :] * ROWS + lane
        return [info[block : block + 1, :] * DOC_STEP + base + block * BLK for block in range(2)]

    own_key = jnp.concatenate([held[core, 0, 0:BLK, :], held[core, 0, BLK : 2 * BLK, :]], axis=1)
    own_value = with_ones(held[core, 0, KSEG:PIECE, :])
    own_line = jnp.concatenate(line_of(core, 0), axis=1)
    inside = []
    for block in range(2):
        low, high, causal = (jnp.broadcast_to(bounds[block][i : i + 1, :], (BLK, BLK)) for i in range(3))
        pos = me * ROWS + block * BLK + iota((BLK, BLK), 0)
        end = high * BLK + (BLK - 1)
        end = jnp.where(causal == 0, end, jnp.minimum(end, pos)) + row_seg[block] * DOC_STEP
        start = low * BLK + row_seg[block] * DOC_STEP
        wide = jnp.broadcast_to(own_line, (BLK, ROWS))
        inside.append(
            (wide >= jnp.concatenate([start, start], axis=1)) & (wide <= jnp.concatenate([end, end], axis=1))
        )
    hidden = jnp.where(jnp.concatenate(inside, axis=0), 0.0, MASKED)
    for part_at in range(GROUP):
        rows = slice(part_at * ROWS, (part_at + 1) * ROWS)
        turn_hidden = by_turn(hidden, part_at // 2)
        score = exact(scaled[rows, 0:HD], own_key)
        score = jnp.where(jnp.concatenate([turn_hidden, turn_hidden], axis=0) < 0.0, MASKED, score)
        new = jnp.broadcast_to(jnp.max(score, axis=1, keepdims=True), (ROWS, HD))
        top[rows, :] = new
        expo = jnp.concatenate(
            [jnp.exp2((score[:, at * BLK : (at + 1) * BLK] - new) * SCALE).astype(jnp.bfloat16) for at in range(2)],
            axis=1,
        )
        total[rows, :] = exact(expo, own_value)

    def attend(*work):
        ready = []
        for pieces, turns in work:
            key_parts, value_parts = [], []
            for role, index in pieces:
                blocks = []
                for block, line in enumerate(line_of(role, index)):
                    spot = jnp.broadcast_to(line, (CLASSES, BLK))
                    seen = (spot >= class_from) & (spot <= class_to)
                    extra = jnp.where(seen, 0.0, MASKED).astype(jnp.bfloat16)
                    blocks.append(
                        jnp.concatenate([held[role, index, block * BLK : (block + 1) * BLK, :], extra], axis=0)
                    )
                key_parts.append(jnp.concatenate(blocks, axis=1))
                value_parts.append(with_ones(held[role, index, KSEG:PIECE, :]))
            value_all = jnp.concatenate(value_parts, axis=0)
            for part_at in [2 * turn + half for turn in turns for half in range(2)]:
                rows = slice(part_at * ROWS, (part_at + 1) * ROWS)
                scores = []
                for key in key_parts:
                    score = exact(scaled[rows, 0 : HD + CLASSES], key)
                    scores += [score[:, 0:BLK], score[:, BLK : 2 * BLK]]
                ready.append((rows, scores, value_all))
        for rows, scores, value_all in ready:
            largest = functools.reduce(jnp.maximum, scores)
            old = top[rows, :]
            new = jnp.maximum(old, jnp.max(largest, axis=1, keepdims=True))
            top[rows, :] = new
            factor = jnp.exp2((old - new) * SCALE)
            expo = jnp.concatenate(
                [jnp.exp2((score - new) * SCALE).astype(jnp.bfloat16) for score in scores], axis=1
            )
            added = exact(expo, value_all)
            total[rows, 0:HD] = total[rows, 0:HD] * factor + added[:, 0:HD]
            total[rows, HD : 2 * HD] = total[rows, HD : 2 * HD] * factor + added[:, HD : 2 * HD]

    def block_core(at):
        return jnp.where((at % 16) // 8 == 0, core, other)

    came = iota((BLK, MIXED), 1)
    expand = one_hot(iota((BLK, MIXED), 0) == 2 * (2 * (came // 16) + block_core(came)) + core)
    owner_rows = jnp.broadcast_to(owner[...].astype(jnp.float32), (8, BLK)).astype(jnp.bfloat16)
    owner_of = exact(owner_rows, expand)[0:1, :].astype(jnp.int32)
    code_in = owner_of * 8 + iota((1, MIXED), 1) % 8
    leaves = iota((MIXED, BLK), 0)
    code_out = (2 * (leaves // 16) + block_core(leaves)) * 8 + leaves % 8
    for at in range(MIXED // BLK):
        columns = slice(at * BLK, (at + 1) * BLK)
        mix[:, columns] = one_hot(code_out == jnp.broadcast_to(code_in[:, columns], (MIXED, BLK)))

    at_out, at_in = iota((ROWS, ROWS), 0), iota((ROWS, ROWS), 1)
    shuffle[0] = one_hot(at_in == (at_out % 8) * TURN + at_out // 8)
    shuffle[1] = one_hot(at_in == (at_out % TURN) * 8 + ((at_out % 64) // TURN) * GROUP + at_out // 64)

    start = (2 * CHIPS - 1) % BATCH
    steps = (2 * CHIPS - 1) // BATCH
    reached = [min(CHIPS - 1, (start + BATCH * step) // 2 + LOOKAHEAD) for step in range(steps)] + [CHIPS - 1]

    def events(step, low, high):
        if high - low == 1:
            indices = tuple(range(reached[low] + 1, reached[low + 1] + 1))
            if indices:
                forward(indices)
            return
        middle = (low + high) // 2

        @pl.when(step < middle)
        def _():
            events(step, low, middle)

        @pl.when(step >= middle)
        def _():
            events(step, middle, high)

    def used(at):
        own = at % 2
        return (core + 1 + own) % 2, (at + own) // 2

    def take(at):
        role, index = used(at)

        @pl.when(at % 2 == 0)
        def _():
            copy((role, index), "all", 0, index, me).wait_recv()

        return role, index

    def batch(step, get):
        return [get(start + BATCH * step + each) for each in range(BATCH)]

    forward(tuple(range(1, reached[0] + 1)))
    attend(([take(jnp.int32(at)) for at in range(start)], (0, 1)))

    def first_half(step, carry):
        events(step, 0, steps)
        attend((batch(step, take), (0,)))
        return carry

    def both_halves(step, carry):
        events(step, 0, steps)
        attend((batch(step, take), (0,)), (batch(step - LAG, used), (1,)))
        return carry

    def second_half(step, carry):
        attend((batch(step, used), (1,)))
        return carry

    lax.fori_loop(0, LAG, first_half, 0)
    lax.fori_loop(LAG, steps, both_halves, 0)

    def swap(turn, way):
        return pltpu.make_async_remote_copy(
            src_ref=swap_out.at[way, turn], dst_ref=swap_in.at[way, turn],
            send_sem=swap_send.at[way, turn], recv_sem=swap_recv.at[way, turn],
            device_id=sibling, device_id_type=MESH,
        )

    def spread(turn, way):
        target = spread_in if way == 0 else back_in

        def one(step, carry):
            there = ctx_of((place.x + step // NZ) % NX, (place.z + step % NZ) % NZ, core)
            pltpu.make_async_remote_copy(
                src_ref=spread_out.at[way, turn, there // CORES], dst_ref=target.at[turn, place.chip_here],
                send_sem=spread_send.at[way, turn], recv_sem=spread_recv.at[way, turn],
                device_id=place.device(there), device_id_type=MESH,
            ).start()
            return carry

        lax.fori_loop(1, CHIPS, one, 0)
        target[turn, place.chip_here] = spread_out[way, turn, place.chip_here]

    def spread_arrived(turn, way):
        target = spread_in if way == 0 else back_in
        many = target.at[turn, pl.ds(0, CHIPS - 1)]
        pltpu.make_async_copy(many, many, spread_recv.at[way, turn]).wait()

    def spread_sent(turn, way):
        many = spread_out.at[way, turn, pl.ds(0, CHIPS - 1)]
        pltpu.make_async_copy(many, many, spread_send.at[way, turn]).wait()

    def close(turn):
        done = [
            (total[rows, 0:HD] / total[rows, HD : 2 * HD]).astype(jnp.bfloat16)
            for rows in (rows_of(turn, head) for head in range(GROUP))
        ]
        for block in range(2):
            starts = [block * 2 * TURN + side * TURN for side in range(2)]
            planes = [done[head][start : start + TURN, :] for start in starts for head in range(GROUP)]
            owned[turn, block] = exact(shuffle[0], jnp.concatenate(planes, axis=0)).astype(jnp.bfloat16)
        swap_out[0, turn] = owned[turn, other]
        swap(turn, 0).start()

    def eights(rows):
        return rows.astype(jnp.float32).reshape(CHIPS, 8, HD)

    def deal(turn):
        swap(turn, 0).wait_recv()
        both = jnp.concatenate([eights(owned[turn, core]), eights(swap_in[0, turn])], axis=1)
        spread_out[0, turn] = both.astype(jnp.bfloat16)
        spread(turn, 0)

    def reorder(turn):
        spread_arrived(turn, 0)
        came_rows = spread_in[turn].reshape(MIXED, HD)
        spread_out[1, turn] = exact(mix[...], came_rows).astype(jnp.bfloat16).reshape(CHIPS, 16, HD)
        spread(turn, 1)

    def collect(turn):
        spread_arrived(turn, 1)
        landed = back_in[turn].astype(jnp.float32)
        owned[turn, core] = landed[:, 0:8, :].reshape(ROWS, HD).astype(jnp.bfloat16)
        swap_out[1, turn] = landed[:, 8:16, :].reshape(ROWS, HD).astype(jnp.bfloat16)
        swap(turn, 1).start()

    def give(turn, message):
        way = 1 if message % 2 == 0 else -1
        side = (0, 1, 1, 0, 0, 1)[message]
        dest = place.plane(2 if message < 2 else way)
        if message < 2:
            target = first_in.at[turn, message]
        else:
            target = last_in.at[turn, message % 2, side]
        return pltpu.make_async_remote_copy(
            src_ref=part.at[turn, dest, side], dst_ref=target,
            send_sem=sum_send.at[turn, message], recv_sem=sum_recv.at[turn, message],
            device_id={"ctx": me, "head": place.plane(way)}, device_id_type=MESH,
        )

    def project(turn):
        swap(turn, 1).wait_recv()
        owned[turn, other] = swap_in[1, turn]
        lefts = []
        for block in range(2):
            sorted_rows = exact(shuffle[1], owned[turn, block]).astype(jnp.bfloat16)
            lefts.append(jnp.concatenate([sorted_rows[64 * head : 64 * (head + 1), :] for head in range(GROUP)], axis=1))
        left = jnp.concatenate(lefts, axis=0)
        for side in range(2):
            for at in range(2):
                start = side * HALF + at * (HALF // 2)
                product = exact(left, proj[:, start : start + HALF // 2]).astype(jnp.bfloat16)
                for dest in range(HEADS):
                    part[turn, dest, side, :, at * (HALF // 2) : (at + 1) * (HALF // 2)] = product[
                        dest * TURN : (dest + 1) * TURN, :
                    ]
        for message in range(4):
            give(turn, message).start()
    def relay(turn):
        for message in (4, 5):
            way = 1 if message == 4 else -1
            side = message - 4
            give(turn, message - 4).wait_recv()
            dest = place.plane(way)
            merged = part[turn, dest, side].astype(jnp.float32) + first_in[turn, side].astype(jnp.float32)
            part[turn, dest, side] = merged.astype(jnp.bfloat16)
            give(turn, message).start()

    def finish(turn):
        for message in range(2, 6):
            give(turn, message).wait_recv()
        for side in range(2):
            summed = part[turn, place.head, side].astype(jnp.float32)
            for way in range(2):
                summed = summed + last_in[turn, way, side].astype(jnp.float32)
            out[turn * TURN : (turn + 1) * TURN, side * HALF : (side + 1) * HALF] = summed.astype(jnp.bfloat16)

    middle = steps - LAG + 1
    close(0)
    lax.fori_loop(steps - LAG, middle, second_half, 0)
    deal(0)
    lax.fori_loop(middle, steps, second_half, 0)
    close(1)
    reorder(0)
    deal(1)
    loads[6].wait()
    collect(0)
    project(0)
    reorder(1)
    relay(0)
    collect(1)
    project(1)
    relay(1)
    finish(0)

    for role in range(2):

        @pl.when(core == role)
        def _(role=role):
            for index in range(CHIPS):
                for each in sends(role, index):
                    each.wait_send()

    finish(1)

    for turn in range(2):
        for way in range(2):
            swap(turn, way).wait_send()
            spread_sent(turn, way)
        for message in range(6):
            give(turn, message).wait_send()


def local(queries, keys, values, segments, block_ranges, owner, out_proj):
    anywhere = pl.BlockSpec(memory_space=pltpu.HBM)
    bf16, i32, f32 = jnp.bfloat16, jnp.int32, jnp.float32
    dma = pltpu.SemaphoreType.DMA
    return pl.pallas_call(
        kernel,
        out_shape=jax.ShapeDtypeStruct((ROWS // HEADS, WIDE), bf16),
        in_specs=[anywhere] * 7,
        out_specs=pl.BlockSpec(memory_space=pltpu.VMEM),
        scratch_shapes=[
            pltpu.VMEM((ROWS, GROUP * HD), bf16),
            pltpu.VMEM((ROWS, HD), bf16),
            pltpu.VMEM((2, BLK), i32),
            pltpu.VMEM((3, 2 * CTX), i32),
            pltpu.VMEM((1, 2 * CTX), i32),
            pltpu.VMEM((GROUP * HD, WIDE), bf16),
            dma((7,)),
            pltpu.VMEM((2, CHIPS, PIECE, HD), bf16),
            pltpu.VMEM((GROUP * ROWS, 2 * HD), bf16),
            pltpu.VMEM((GROUP * ROWS, 2 * HD), f32),
            pltpu.VMEM((GROUP * ROWS, HD), f32),
            dma((2, CHIPS, 2)),
            dma((CHIPS, 5)),
            pltpu.VMEM((2, ROWS, ROWS), bf16),
            pltpu.VMEM((2, 2, ROWS, HD), bf16),
            pltpu.VMEM((2, 2, ROWS, HD), bf16),
            pltpu.VMEM((2, 2, CHIPS, 16, HD), bf16),
            pltpu.VMEM((2, CHIPS, 16, HD), bf16),
            pltpu.VMEM((2, CHIPS, 16, HD), bf16),
            pltpu.VMEM((MIXED, MIXED), bf16),
            pltpu.VMEM((2, 2, ROWS, HD), bf16),
            dma((2, 2)),
            dma((2, 2)),
            dma((2, 2)),
            dma((2, 2)),
            pltpu.VMEM((2, HEADS, 2, TURN, HALF), bf16),
            pltpu.VMEM((2, 2, TURN, HALF), bf16),
            pltpu.VMEM((2, 2, 2, TURN, HALF), bf16),
            dma((2, 6)),
            dma((2, 6)),
        ],
        compiler_params=pltpu.CompilerParams(
            collective_id=0, has_side_effects=True, vmem_limit_bytes=60 << 20
        ),
        cost_estimate=pl.CostEstimate(
            flops=4 * GROUP * ROWS * ROWS * CTX * HD,
            bytes_accessed=GROUP * HD * WIDE * 2,
            transcendentals=GROUP * ROWS * ROWS * CTX,
        ),
        name="attend_and_project",
    )(
        queries, keys, values, segments.reshape(2, BLK), block_ranges.T, owner.reshape(1, 2 * CTX), out_proj
    )


def solution(mesh):
    return jax.shard_map(
        local,
        mesh=mesh,
        in_specs=(
            P("ctx", "head"),
            P("ctx", "head"),
            P("ctx", "head"),
            P("ctx"),
            P(),
            P(),
            P("head", None),
        ),
        out_specs=P(("ctx", "head"), None),
        check_vma=False,
    )
```

```python
import functools
import math

import jax
import jax.numpy as jnp
from jax import lax
from jax.experimental import pallas as pl
from jax.experimental.pallas import tpu as pltpu
from jax.sharding import PartitionSpec as P

MESH = pl.DeviceIdType.MESH
HD = 128
BLK = 128
GROUP = 4
NX, NZ, CORES = 4, 8, 2
CTX = NX * NZ * CORES
HEADS = 4
ROWS = 256
KSEG = ROWS + 16
PIECE = KSEG + ROWS
CHIPS = NX * NZ
WIDE = 4096
HALF = WIDE // 2
TURN = 32
MIXED = CHIPS * 16
BIAS = -(2**31)
LOOKAHEAD = 3
EARLY = 13
LAG = 8
MASKED = -1e30
SCALE = math.log2(math.e) / math.sqrt(HD)


def ctx_of(x, z, core):
    return (x * NZ + z) * CORES + core


def ring_offsets(size):
    half = size // 2
    found = [0]
    for step in range(1, half):
        found += [step, -step]
    return found + [half]


def piece_order(size_a, size_b):
    pieces = [(da, db) for da in ring_offsets(size_a) for db in ring_offsets(size_b)]
    return sorted(pieces, key=lambda piece: abs(piece[0]) + abs(piece[1]))


ORDERS = (piece_order(NX, NZ), piece_order(NZ, NX))


class Place:
    def __init__(self):
        ctx = lax.axis_index("ctx")
        self.ctx = ctx
        self.head = lax.axis_index("head")
        self.core = ctx % CORES
        self.z = (ctx // CORES) % NZ
        self.x = ctx // (CORES * NZ)
        self.chip_here = ctx // CORES

    def chip(self, dx, dz, core):
        return ctx_of((self.x + dx + NX) % NX, (self.z + dz + NZ) % NZ, core)

    def device(self, ctx):
        return {"ctx": ctx, "head": self.head}

    def plane(self, step):
        return (self.head + step) % HEADS


def iota(shape, dim):
    return lax.broadcasted_iota(jnp.int32, shape, dim)


def one_hot(mask):
    return jnp.where(mask, 1.0, 0.0).astype(jnp.bfloat16)


def exact(left, right):
    return jnp.dot(left, right, preferred_element_type=jnp.float32)


def kernel(
    queries_hbm, keys_hbm, values_hbm, segs_hbm, ranges_hbm, owner_hbm, proj_hbm, out,
    queries, keys, segs, ranges, owner, proj, load_sem,
    held, scaled, total, top, first, width, recv_sem, send_sem,
    shuffle, swap_out, swap_in, spread_out, spread_in, back_in, mix, owned, swap_send, swap_recv, spread_send, spread_recv,
    part, first_in, last_in, sum_send, sum_recv,
):
    place = Place()
    me, core, other = place.ctx, place.core, 1 - place.core

    loads = [
        pltpu.make_async_copy(source, target, load_sem.at[at])
        for at, (source, target) in enumerate(
            (
                (keys_hbm, keys),
                (segs_hbm, segs),
                (values_hbm, held.at[core, 0, pl.ds(KSEG, ROWS), :]),
                (queries_hbm, queries),
                (ranges_hbm, ranges),
                (owner_hbm, owner),
                (proj_hbm, proj),
            )
        )
    ]
    for load in loads:
        load.start()

    barrier = pltpu.get_barrier_semaphore()
    sibling = place.device(place.chip(0, 0, other))

    def greet(step, carry):
        target = place.device(place.chip(step // NZ, step % NZ, core))
        pl.semaphore_signal(barrier, inc=1, device_id=target, device_id_type=MESH)
        return carry

    lax.fori_loop(1, CHIPS, greet, 0)
    around = [sibling] + [{"ctx": me, "head": place.plane(step)} for step in (1, -1)]
    for device in around:
        pl.semaphore_signal(barrier, inc=1, device_id=device, device_id_type=MESH)

    for load in loads[:3]:
        load.wait()
    for block in range(2):
        turned = jnp.transpose(keys[block * BLK : (block + 1) * BLK, :].astype(jnp.float32))
        held[core, 0, block * BLK : (block + 1) * BLK, :] = turned.astype(jnp.bfloat16)
    seg_rows = segs[...].astype(jnp.float32)
    held[core, 0, ROWS:KSEG, :] = jnp.concatenate(
        [seg_rows, jnp.full((1, BLK), me, jnp.int32).astype(jnp.float32), jnp.zeros((13, BLK), jnp.float32)], axis=0
    ).astype(jnp.bfloat16)
    pl.semaphore_wait(barrier, CHIPS - 1 + len(around))

    parts = {"all": (0, PIECE, 0), "keys": (0, KSEG, 0), "values": (KSEG, ROWS, 1)}

    def copy(piece, name, kind, at, device):
        role, index = piece
        start, size, which = parts[name]
        return pltpu.make_async_remote_copy(
            src_ref=held.at[role, index, pl.ds(start, size), :],
            dst_ref=held.at[role, at, pl.ds(start, size), :],
            send_sem=send_sem.at[index, kind], recv_sem=recv_sem.at[role, at, which],
            device_id=place.device(device), device_id_type=MESH,
        )

    def sends(role, index):
        order = ORDERS[role]
        sizes = (NX, NZ) if role == 0 else (NZ, NX)
        offsets = order[index]
        found = []

        def go(name, axis, way):
            moved = list(offsets)
            moved[axis] -= way
            for each in range(2):
                if moved[each] <= -sizes[each] // 2:
                    moved[each] += sizes[each]
            step = [0, 0]
            step[axis] = way
            dx, dz = step if role == 0 else step[::-1]
            kind = 2 * axis + (0 if way > 0 else 1)
            found.append(copy((role, index), name, kind, order.index(tuple(moved)), place.chip(dx, dz, role)))

        for axis in range(2):
            if axis == 0 and offsets[1] != 0:
                continue
            offset, half = offsets[axis], sizes[axis] // 2
            if offset == 0:
                go("all", axis, 1)
                go("all", axis, -1)
            elif abs(offset) < half:
                name = "all" if abs(offset) < half - 1 else ("keys" if offset > 0 else "values")
                go(name, axis, -1 if offset > 0 else 1)
        found.append(copy((role, index), "all", 4, index, place.chip(0, 0, 1 - role)))
        return found

    def arrive(role, index):
        da, db = ORDERS[role][index]
        sizes = (NX, NZ) if role == 0 else (NZ, NX)
        if index == 0:
            return
        halves = db == sizes[1] // 2 or (db == 0 and da == sizes[0] // 2)
        for name in ("keys", "values") if halves else ("all",):
            copy((role, index), name, 0, index, me).wait_recv()

    def forward(indices):
        for role in range(2):

            @pl.when(core == role)
            def _(role=role):
                for index in indices:
                    arrive(role, index)
                    for each in sends(role, index):
                        each.start()

    forward((0,))

    for load in loads[3:6]:
        load.wait()

    def block_core(at):
        return jnp.where((at % 16) // 8 == 0, core, other)

    came = iota((BLK, MIXED), 1)
    expand = one_hot(iota((BLK, MIXED), 0) == 2 * (2 * (came // 16) + block_core(came)) + core)
    owner_rows = jnp.broadcast_to(owner[...].astype(jnp.float32), (8, BLK)).astype(jnp.bfloat16)
    owner_of = exact(owner_rows, expand)[0:1, :].astype(jnp.int32)
    code_in = owner_of * 8 + iota((1, MIXED), 1) % 8
    leaves = iota((MIXED, BLK), 0)
    code_out = (2 * (leaves // 16) + block_core(leaves)) * 8 + leaves % 8
    for at in range(MIXED // BLK):
        columns = slice(at * BLK, (at + 1) * BLK)
        mix[:, columns] = one_hot(code_out == jnp.broadcast_to(code_in[:, columns], (MIXED, BLK)))

    at_out, at_in = iota((ROWS, ROWS), 0), iota((ROWS, ROWS), 1)
    shuffle[0] = one_hot(at_in == (at_out % 8) * TURN + at_out // 8)
    shuffle[1] = one_hot(at_in == (at_out % TURN) * 8 + ((at_out % 64) // TURN) * GROUP + at_out // 64)

    def swap(turn, way):
        return pltpu.make_async_remote_copy(
            src_ref=swap_out.at[way, turn], dst_ref=swap_in.at[way, turn],
            send_sem=swap_send.at[way, turn], recv_sem=swap_recv.at[way, turn],
            device_id=sibling, device_id_type=MESH,
        )

    def height(turn, way):
        return 32 if turn == 0 and way == 0 else 16

    def spread(turn, way):
        target = spread_in if way == 0 else back_in
        tall = height(turn, way)

        def one(step, carry):
            there = ctx_of((place.x + step // NZ) % NX, (place.z + step % NZ) % NZ, core)
            pltpu.make_async_remote_copy(
                src_ref=spread_out.at[way, turn, there // CORES, pl.ds(0, tall)],
                dst_ref=target.at[turn, place.chip_here, pl.ds(0, tall)],
                send_sem=spread_send.at[way, turn], recv_sem=spread_recv.at[way, turn],
                device_id=place.device(there), device_id_type=MESH,
            ).start()
            return carry

        lax.fori_loop(1, CHIPS, one, 0)
        target[turn, place.chip_here] = spread_out[way, turn, place.chip_here]

    def spread_arrived(turn, way):
        target = spread_in if way == 0 else back_in
        many = target.at[turn, pl.ds(0, CHIPS - 1), pl.ds(0, height(turn, way))]
        pltpu.make_async_copy(many, many, spread_recv.at[way, turn]).wait()

    def spread_sent(turn, way):
        many = spread_out.at[way, turn, pl.ds(0, CHIPS - 1), pl.ds(0, height(turn, way))]
        pltpu.make_async_copy(many, many, spread_send.at[way, turn]).wait()

    def close(turn):
        for block in range(2):
            starts = [block * BLK + side * 2 * TURN + turn * TURN for side in range(2)]
            planes = [
                queries[start : start + TURN, head * HD : (head + 1) * HD] for start in starts for head in range(GROUP)
            ]
            owned[turn, block] = exact(shuffle[0], jnp.concatenate(planes, axis=0)).astype(jnp.bfloat16)
        swap_out[0, turn, 0:ROWS, :] = owned[turn, other]
        swap_out[0, turn, ROWS:KSEG, :] = held[core, 0, ROWS:KSEG, :]
        swap(turn, 0).start()

    def eights(rows):
        return rows.astype(jnp.float32).reshape(CHIPS, 8, HD)

    def deal(turn):
        swap(turn, 0).wait_recv()
        both = jnp.concatenate([eights(owned[turn, core]), eights(swap_in[0, turn, 0:ROWS, :])], axis=1)
        spread_out[0, turn, :, 0:16, :] = both.astype(jnp.bfloat16)
        if turn == 0:
            theirs = swap_in[0, turn, ROWS:KSEG, :].astype(jnp.float32)
            docs = jnp.concatenate([seg_rows, theirs[0:2, :], jnp.zeros((12, BLK), jnp.float32)], axis=0)
            spread_out[0, turn, :, 16:32, :] = jnp.broadcast_to(docs.astype(jnp.bfloat16)[None], (CHIPS, 16, BLK))
        spread(turn, 0)

    def reorder(turn):
        spread_arrived(turn, 0)
        came_rows = spread_in[turn, :, 0:16, :].reshape(MIXED, HD)
        spread_out[1, turn, :, 0:16, :] = exact(mix[...], came_rows).astype(jnp.bfloat16).reshape(CHIPS, 16, HD)
        spread(turn, 1)

    def collect(turn):
        spread_arrived(turn, 1)
        landed = back_in[turn, :, 0:16, :].astype(jnp.float32)
        owned[turn, core] = landed[:, 0:8, :].reshape(ROWS, HD).astype(jnp.bfloat16)
        swap_out[1, turn, 0:ROWS, :] = landed[:, 8:16, :].reshape(ROWS, HD).astype(jnp.bfloat16)
        swap(turn, 1).start()

    def rows_of(turn, head):
        start = turn * GROUP * BLK + head * BLK
        return slice(start, start + BLK)

    def settle(turn):
        swap(turn, 1).wait_recv()
        owned[turn, other] = swap_in[1, turn, 0:ROWS, :]
        turned = [exact(shuffle[1], owned[turn, block]).astype(jnp.bfloat16) for block in range(2)]
        for head in range(GROUP):
            scaled[rows_of(turn, head), :] = jnp.concatenate(
                [turned[block][64 * head : 64 * (head + 1), :] for block in range(2)], axis=0
            )

    def intervals():
        docs = spread_in[0, :, 16:32, :].astype(jnp.float32)
        real = iota((16, BLK), 0) < 4
        begins = []
        for doc in (1.0, 2.0):
            before = jnp.sum(jnp.where(docs < doc, 1.0, 0.0), axis=0)
            before = jnp.sum(jnp.where(real, before, 0.0), axis=0, keepdims=True)
            begins.append(jnp.sum(before, axis=1, keepdims=True).astype(jnp.int32))
        one, two = (jnp.broadcast_to(begin, (64, BLK)) for begin in begins)
        lane = iota((1, BLK), 1)
        for block in range(2):
            mine = (owner[...] == me) & (lane % 2 == block)

            def pick(array):
                chosen = jnp.where(mine, array, 0).astype(jnp.float32)
                chosen = jnp.sum(chosen, axis=1, keepdims=True).astype(jnp.int32)
                return jnp.broadcast_to(chosen, (64, BLK))

            wanted = pick(lane)
            low, high, causal = (pick(ranges[at : at + 1, :]) for at in range(3))
            for turn in range(2):
                at = iota((64, BLK), 0)
                pos = wanted * BLK + (at // TURN) * 2 * TURN + turn * TURN + at % TURN
                start = jnp.maximum(low * BLK, jnp.where(pos >= two, two, jnp.where(pos >= one, one, 0)))
                end = jnp.where(pos < one, one, jnp.where(pos < two, two, CTX * ROWS)) - 1
                end = jnp.minimum(end, high * BLK + (BLK - 1))
                end = jnp.where(causal == 0, end, jnp.minimum(end, pos))
                first[turn, block * 64 : (block + 1) * 64, :] = jnp.int32(BIAS) - start
                width[turn, block * 64 : (block + 1) * 64, :] = (end - start + 1) + jnp.int32(BIAS)

    def with_ones(value):
        return jnp.concatenate([value, jnp.ones_like(value)], axis=1)

    def attend(*work):
        ready = []
        lane = iota((1, BLK), 1)
        for pieces, turns in work:
            key_parts, value_parts, lines = [], [], []
            for role, index in pieces:
                key_parts.append(
                    jnp.concatenate([held[role, index, 0:BLK, :], held[role, index, BLK : 2 * BLK, :]], axis=1)
                )
                value_parts.append(with_ones(held[role, index, KSEG:PIECE, :]))
                info = held[role, index, ROWS:KSEG, :].astype(jnp.float32).astype(jnp.int32)
                lines += [info[2:3, :] * ROWS + lane + block * BLK for block in range(2)]
            value_all = jnp.concatenate(value_parts, axis=0)
            for turn in turns:
                inside = [line + first[turn] < width[turn] for line in lines]
                for part_at in (2 * turn, 2 * turn + 1):
                    rows = slice(part_at * ROWS, (part_at + 1) * ROWS)
                    scores = []
                    for at, key in enumerate(key_parts):
                        score = exact(scaled[rows, :], key)
                        for block in range(2):
                            columns = slice(block * BLK, (block + 1) * BLK)
                            scores.append(
                                jnp.concatenate(
                                    [
                                        jnp.where(inside[2 * at + block], score[half : half + BLK, columns], MASKED)
                                        for half in (0, BLK)
                                    ],
                                    axis=0,
                                )
                            )
                    ready.append((rows, scores, value_all))
        for rows, scores, value_all in ready:
            largest = functools.reduce(jnp.maximum, scores)
            old = top[rows, :]
            new = jnp.maximum(old, jnp.max(largest, axis=1, keepdims=True))
            top[rows, :] = new
            factor = jnp.exp2((old - new) * SCALE)
            expo = jnp.concatenate(
                [jnp.exp2((score - new) * SCALE).astype(jnp.bfloat16) for score in scores], axis=1
            )
            added = exact(expo, value_all)
            total[rows, 0:HD] = total[rows, 0:HD] * factor + added[:, 0:HD]
            total[rows, HD : 2 * HD] = total[rows, HD : 2 * HD] * factor + added[:, HD : 2 * HD]

    steps = CHIPS // 2
    reached = [min(CHIPS - 1, max(EARLY, 2 * step + 1 + LOOKAHEAD)) for step in range(steps)]

    def events(step, low, high):
        if high - low == 1:
            indices = tuple(range((reached[low - 1] if low else EARLY) + 1, reached[low] + 1))
            if indices:
                forward(indices)
            return
        middle = (low + high) // 2

        @pl.when(step < middle)
        def _():
            events(step, low, middle)

        @pl.when(step >= middle)
        def _():
            events(step, middle, high)

    def used(step):
        return [(role, 2 * step + each) for role in (core, other) for each in range(2)]

    def take(step):
        pieces = used(step)
        for role, index in pieces[2:]:
            copy((role, index), "all", 0, index, me).wait_recv()
        return pieces

    def first_half(step, carry):
        events(step, 0, steps)
        attend((take(step), (0,)))
        return carry

    def both_halves(step, carry):
        events(step, 0, steps)
        attend((take(step), (0,)), (used(step - LAG), (1,)))
        return carry

    def second_half(step, carry):
        attend((used(step), (1,)))
        return carry

    def give(turn, message):
        way = 1 if message % 2 == 0 else -1
        side = (0, 1, 1, 0, 0, 1)[message]
        dest = place.plane(2 if message < 2 else way)
        if message < 2:
            target = first_in.at[turn, message]
        else:
            target = last_in.at[turn, message % 2, side]
        return pltpu.make_async_remote_copy(
            src_ref=part.at[turn, dest, side], dst_ref=target,
            send_sem=sum_send.at[turn, message], recv_sem=sum_recv.at[turn, message],
            device_id={"ctx": me, "head": place.plane(way)}, device_id_type=MESH,
        )

    def project(turn):
        left = jnp.concatenate(
            [
                (total[rows, 0:HD] / total[rows, HD : 2 * HD]).astype(jnp.bfloat16)
                for rows in (rows_of(turn, head) for head in range(GROUP))
            ],
            axis=1,
        )
        for side in range(2):
            for at in range(2):
                start = side * HALF + at * (HALF // 2)
                product = exact(left, proj[:, start : start + HALF // 2]).astype(jnp.bfloat16)
                for dest in range(HEADS):
                    part[turn, dest, side, :, at * (HALF // 2) : (at + 1) * (HALF // 2)] = product[
                        dest * TURN : (dest + 1) * TURN, :
                    ]
        for message in range(4):
            give(turn, message).start()
    def relay(turn):
        for message in (4, 5):
            way = 1 if message == 4 else -1
            side = message - 4
            give(turn, message - 4).wait_recv()
            dest = place.plane(way)
            merged = part[turn, dest, side].astype(jnp.float32) + first_in[turn, side].astype(jnp.float32)
            part[turn, dest, side] = merged.astype(jnp.bfloat16)
            give(turn, message).start()

    def finish(turn):
        for message in range(2, 6):
            give(turn, message).wait_recv()
        for side in range(2):
            summed = part[turn, place.head, side].astype(jnp.float32)
            for way in range(2):
                summed = summed + last_in[turn, way, side].astype(jnp.float32)
            out[turn * TURN : (turn + 1) * TURN, side * HALF : (side + 1) * HALF] = summed.astype(jnp.bfloat16)

    middle = steps - LAG + 1
    top[...] = jnp.full(top.shape, MASKED, jnp.float32)
    total[...] = jnp.zeros(total.shape, jnp.float32)
    close(0)
    close(1)
    deal(0)
    deal(1)
    forward(range(1, 5))
    reorder(0)
    reorder(1)
    forward(range(5, 12))
    intervals()
    collect(0)
    collect(1)
    forward(range(12, EARLY + 1))
    settle(0)
    settle(1)

    lax.fori_loop(0, LAG, first_half, 0)
    lax.fori_loop(LAG, steps, both_halves, 0)
    loads[6].wait()
    project(0)
    middle = steps - LAG + (LAG + 1) // 2
    lax.fori_loop(steps - LAG, middle, second_half, 0)
    relay(0)
    lax.fori_loop(middle, steps, second_half, 0)
    project(1)
    relay(1)
    finish(0)

    for role in range(2):

        @pl.when(core == role)
        def _(role=role):
            for index in range(CHIPS):
                for each in sends(role, index):
                    each.wait_send()

    finish(1)

    for turn in range(2):
        for way in range(2):
            swap(turn, way).wait_send()
            spread_sent(turn, way)
        for message in range(6):
            give(turn, message).wait_send()


def local(queries, keys, values, segments, block_ranges, owner, out_proj):
    anywhere = pl.BlockSpec(memory_space=pltpu.HBM)
    bf16, i32, f32 = jnp.bfloat16, jnp.int32, jnp.float32
    dma = pltpu.SemaphoreType.DMA
    return pl.pallas_call(
        kernel,
        out_shape=jax.ShapeDtypeStruct((ROWS // HEADS, WIDE), bf16),
        in_specs=[anywhere] * 7,
        out_specs=pl.BlockSpec(memory_space=pltpu.VMEM),
        scratch_shapes=[
            pltpu.VMEM((ROWS, GROUP * HD), bf16),
            pltpu.VMEM((ROWS, HD), bf16),
            pltpu.VMEM((2, BLK), i32),
            pltpu.VMEM((3, 2 * CTX), i32),
            pltpu.VMEM((1, 2 * CTX), i32),
            pltpu.VMEM((GROUP * HD, WIDE), bf16),
            dma((7,)),
            pltpu.VMEM((2, CHIPS, PIECE, HD), bf16),
            pltpu.VMEM((GROUP * ROWS, HD), bf16),
            pltpu.VMEM((GROUP * ROWS, 2 * HD), f32),
            pltpu.VMEM((GROUP * ROWS, HD), f32),
            pltpu.VMEM((2, BLK, BLK), i32),
            pltpu.VMEM((2, BLK, BLK), i32),
            dma((2, CHIPS, 2)),
            dma((CHIPS, 5)),
            pltpu.VMEM((2, ROWS, ROWS), bf16),
            pltpu.VMEM((2, 2, KSEG, HD), bf16),
            pltpu.VMEM((2, 2, KSEG, HD), bf16),
            pltpu.VMEM((2, 2, CHIPS, 32, HD), bf16),
            pltpu.VMEM((2, CHIPS, 32, HD), bf16),
            pltpu.VMEM((2, CHIPS, 32, HD), bf16),
            pltpu.VMEM((MIXED, MIXED), bf16),
            pltpu.VMEM((2, 2, ROWS, HD), bf16),
            dma((2, 2)),
            dma((2, 2)),
            dma((2, 2)),
            dma((2, 2)),
            pltpu.VMEM((2, HEADS, 2, TURN, HALF), bf16),
            pltpu.VMEM((2, 2, TURN, HALF), bf16),
            pltpu.VMEM((2, 2, 2, TURN, HALF), bf16),
            dma((2, 6)),
            dma((2, 6)),
        ],
        compiler_params=pltpu.CompilerParams(
            collective_id=0, has_side_effects=True, vmem_limit_bytes=60 << 20
        ),
        cost_estimate=pl.CostEstimate(
            flops=4 * GROUP * ROWS * ROWS * CTX * HD,
            bytes_accessed=GROUP * HD * WIDE * 2,
            transcendentals=GROUP * ROWS * ROWS * CTX,
        ),
        name="attend_and_project",
    )(
        queries, keys, values, segments.reshape(2, BLK), block_ranges.T, owner.reshape(1, 2 * CTX), out_proj
    )


def solution(mesh):
    return jax.shard_map(
        local,
        mesh=mesh,
        in_specs=(
            P("ctx", "head"),
            P("ctx", "head"),
            P("ctx", "head"),
            P("ctx"),
            P(),
            P(),
            P("head", None),
        ),
        out_specs=P(("ctx", "head"), None),
        check_vma=False,
    )
```

```python
import functools
import math

import jax
import jax.numpy as jnp
from jax import lax
from jax.experimental import pallas as pl
from jax.experimental.pallas import tpu as pltpu
from jax.sharding import PartitionSpec as P

MESH = pl.DeviceIdType.MESH
HD = 128
BLK = 128
GROUP = 4
NX, NZ, CORES = 4, 8, 2
CTX = NX * NZ * CORES
HEADS = 4
ROWS = 256
KSEG = ROWS + 16
PIECE = KSEG + ROWS
CHIPS = NX * NZ
WIDE = 4096
HALF = WIDE // 2
TURN = 32
MIXED = CHIPS * 16
CLASSES = 16
BATCH = 4
LOOKAHEAD = 3
DOC_STEP = 32768
MASKED = -1e30
SCALE = math.log2(math.e) / math.sqrt(HD)


def ctx_of(x, z, core):
    return (x * NZ + z) * CORES + core


def ring_offsets(size):
    half = size // 2
    found = [0]
    for step in range(1, half):
        found += [step, -step]
    return found + [half]


def piece_order(size_a, size_b):
    pieces = [(da, db) for da in ring_offsets(size_a) for db in ring_offsets(size_b)]
    weights = [2 if size == NX else 3 for size in (size_a, size_b)]
    return sorted(pieces, key=lambda piece: weights[0] * abs(piece[0]) + weights[1] * abs(piece[1]))


ORDERS = (piece_order(NX, NZ), piece_order(NZ, NX))


class Place:
    def __init__(self):
        ctx = lax.axis_index("ctx")
        self.ctx = ctx
        self.head = lax.axis_index("head")
        self.core = ctx % CORES
        self.z = (ctx // CORES) % NZ
        self.x = ctx // (CORES * NZ)
        self.chip_here = ctx // CORES

    def chip(self, dx, dz, core):
        return ctx_of((self.x + dx + NX) % NX, (self.z + dz + NZ) % NZ, core)

    def device(self, ctx):
        return {"ctx": ctx, "head": self.head}

    def plane(self, step):
        return (self.head + step) % HEADS


def iota(shape, dim):
    return lax.broadcasted_iota(jnp.int32, shape, dim)


def one_hot(mask):
    return jnp.where(mask, 1.0, 0.0).astype(jnp.bfloat16)


def exact(left, right):
    return jnp.dot(left, right, preferred_element_type=jnp.float32)


def kernel(
    queries_hbm, keys_hbm, values_hbm, segs_hbm, ranges_hbm, owner_hbm, proj_hbm, out,
    queries, keys, segs, ranges, owner, proj, load_sem,
    held, scaled, total, top, recv_sem, send_sem,
    shuffle, swap_out, swap_in, spread_out, spread_in, back_in, mix, owned, swap_send, swap_recv, spread_send, spread_recv,
    part, first_in, last_in, sum_send, sum_recv,
):
    place = Place()
    me, core, other = place.ctx, place.core, 1 - place.core

    loads = [
        pltpu.make_async_copy(source, target, load_sem.at[at])
        for at, (source, target) in enumerate(
            (
                (keys_hbm, keys),
                (segs_hbm, segs),
                (values_hbm, held.at[core, 0, pl.ds(KSEG, ROWS), :]),
                (queries_hbm, queries),
                (ranges_hbm, ranges),
                (owner_hbm, owner),
                (proj_hbm, proj),
            )
        )
    ]
    for load in loads:
        load.start()

    barrier = pltpu.get_barrier_semaphore()
    sibling = place.device(place.chip(0, 0, other))

    around = [place.device(place.chip(dx, dz, core)) for dx, dz in ((1, 0), (-1, 0), (0, 1), (0, -1))]
    around += [sibling] + [{"ctx": me, "head": place.plane(step)} for step in (1, -1)]
    for device in around:
        pl.semaphore_signal(barrier, inc=1, device_id=device, device_id_type=MESH)

    for load in loads[:3]:
        load.wait()
    for block in range(2):
        turned = jnp.transpose(keys[block * BLK : (block + 1) * BLK, :].astype(jnp.float32))
        held[core, 0, block * BLK : (block + 1) * BLK, :] = turned.astype(jnp.bfloat16)
    seg_rows = segs[...].astype(jnp.float32)
    held[core, 0, ROWS:KSEG, :] = jnp.concatenate(
        [seg_rows, jnp.full((1, BLK), me, jnp.int32).astype(jnp.float32), jnp.zeros((13, BLK), jnp.float32)], axis=0
    ).astype(jnp.bfloat16)
    pl.semaphore_wait(barrier, len(around))

    parts = {"all": (0, PIECE, 0), "keys": (0, KSEG, 0), "values": (KSEG, ROWS, 1)}

    def copy(piece, name, kind, at, device):
        role, index = piece
        start, size, which = parts[name]
        return pltpu.make_async_remote_copy(
            src_ref=held.at[role, index, pl.ds(start, size), :],
            dst_ref=held.at[role, at, pl.ds(start, size), :],
            send_sem=send_sem.at[index, kind], recv_sem=recv_sem.at[role, at, which],
            device_id=place.device(device), device_id_type=MESH,
        )

    def pair_copy(role, index):
        pair = held.at[role, pl.ds(index, 2)]
        return pltpu.make_async_remote_copy(
            src_ref=pair, dst_ref=pair, send_sem=send_sem.at[index, 4], recv_sem=recv_sem.at[role, index, 0],
            device_id=sibling, device_id_type=MESH,
        )

    def sends(role, index):
        order = ORDERS[role]
        sizes = (NX, NZ) if role == 0 else (NZ, NX)
        offsets = order[index]
        found = []

        def go(name, axis, way):
            moved = list(offsets)
            moved[axis] -= way
            for each in range(2):
                if moved[each] <= -sizes[each] // 2:
                    moved[each] += sizes[each]
            step = [0, 0]
            step[axis] = way
            dx, dz = step if role == 0 else step[::-1]
            kind = 2 * axis + (0 if way > 0 else 1)
            found.append(copy((role, index), name, kind, order.index(tuple(moved)), place.chip(dx, dz, role)))

        for axis in range(2):
            if axis == 0 and offsets[1] != 0:
                continue
            offset, half = offsets[axis], sizes[axis] // 2
            if offset == 0:
                go("all", axis, 1)
                go("all", axis, -1)
            elif abs(offset) < half:
                name = "all" if abs(offset) < half - 1 else ("keys" if offset > 0 else "values")
                go(name, axis, -1 if offset > 0 else 1)
        if index in (0, CHIPS - 1):
            found.append(copy((role, index), "all", 4, index, place.chip(0, 0, 1 - role)))
        elif index % 2 == 0:
            found.append(pair_copy(role, index - 1))
        return found

    def arrive(role, index):
        da, db = ORDERS[role][index]
        sizes = (NX, NZ) if role == 0 else (NZ, NX)
        if index == 0:
            return
        halves = db == sizes[1] // 2 or (db == 0 and da == sizes[0] // 2)
        for name in ("keys", "values") if halves else ("all",):
            copy((role, index), name, 0, index, me).wait_recv()

    def forward(indices):
        for role in range(2):

            @pl.when(core == role)
            def _(role=role):
                for index in indices:
                    arrive(role, index)
                    for each in sends(role, index):
                        each.start()

    forward((0,))

    for load in loads[3:6]:
        load.wait()
    lane = iota((1, BLK), 1)
    bounds = []
    for block in range(2):
        picked = jnp.where(lane == 2 * me + block, ranges[...], 0).astype(jnp.float32)
        bounds.append(jnp.sum(picked, axis=1, keepdims=True).astype(jnp.int32))
    row = iota((CLASSES, BLK), 0)
    low, high = (
        jnp.where(
            row < 3,
            jnp.broadcast_to(bounds[0][at : at + 1, :], (CLASSES, BLK)),
            jnp.broadcast_to(bounds[1][at : at + 1, :], (CLASSES, BLK)),
        )
        for at in range(2)
    )
    class_seg = jnp.where(row < 3, row, row - 3) * DOC_STEP
    class_from = low * BLK + class_seg
    class_to = high * BLK + (BLK - 1) + class_seg

    row_seg = [
        jnp.transpose(jnp.broadcast_to(seg_rows[block : block + 1, :], (BLK, BLK))).astype(jnp.int32)
        for block in range(2)
    ]
    row_class = jnp.concatenate([row_seg[0], row_seg[1] + 3], axis=0)
    chosen = one_hot(row_class[:, 0:CLASSES] == iota((ROWS, CLASSES), 1))
    def by_turn(array, turn):
        starts = [block * BLK + side * 2 * TURN + turn * TURN for block in range(2) for side in range(2)]
        return jnp.concatenate([array[start : start + TURN, :] for start in starts], axis=0)

    def rows_of(turn, head):
        start = turn * GROUP * BLK + head * BLK
        return slice(start, start + BLK)

    all_queries = queries[...]
    for turn in range(2):
        turn_queries, turn_chosen = by_turn(all_queries, turn), by_turn(chosen, turn)
        for head in range(GROUP):
            scaled[rows_of(turn, head), 0:HD] = turn_queries[:, head * HD : (head + 1) * HD]
            scaled[rows_of(turn, head), HD : HD + CLASSES] = turn_chosen

    def with_ones(value):
        return jnp.concatenate([value, jnp.ones_like(value)], axis=1)

    def line_of(role, index):
        info = held[role, index, ROWS:KSEG, :].astype(jnp.float32).astype(jnp.int32)
        base = info[2:3, :] * ROWS + lane
        return [info[block : block + 1, :] * DOC_STEP + base + block * BLK for block in range(2)]

    own_key = jnp.concatenate([held[core, 0, 0:BLK, :], held[core, 0, BLK : 2 * BLK, :]], axis=1)
    own_value = with_ones(held[core, 0, KSEG:PIECE, :])
    own_line = jnp.concatenate(line_of(core, 0), axis=1)
    inside = []
    for block in range(2):
        low, high, causal = (jnp.broadcast_to(bounds[block][i : i + 1, :], (BLK, BLK)) for i in range(3))
        pos = me * ROWS + block * BLK + iota((BLK, BLK), 0)
        end = high * BLK + (BLK - 1)
        end = jnp.where(causal == 0, end, jnp.minimum(end, pos)) + row_seg[block] * DOC_STEP
        start = low * BLK + row_seg[block] * DOC_STEP
        wide = jnp.broadcast_to(own_line, (BLK, ROWS))
        inside.append(
            (wide >= jnp.concatenate([start, start], axis=1)) & (wide <= jnp.concatenate([end, end], axis=1))
        )
    hidden = jnp.where(jnp.concatenate(inside, axis=0), 0.0, MASKED)
    for part_at in range(GROUP):
        rows = slice(part_at * ROWS, (part_at + 1) * ROWS)
        turn_hidden = by_turn(hidden, part_at // 2)
        score = exact(scaled[rows, 0:HD], own_key)
        score = jnp.where(jnp.concatenate([turn_hidden, turn_hidden], axis=0) < 0.0, MASKED, score)
        new = jnp.broadcast_to(jnp.max(score, axis=1, keepdims=True), (ROWS, HD))
        top[rows, :] = new
        expo = jnp.concatenate(
            [jnp.exp2((score[:, at * BLK : (at + 1) * BLK] - new) * SCALE).astype(jnp.bfloat16) for at in range(2)],
            axis=1,
        )
        total[rows, :] = exact(expo, own_value)

    def attend(*work):
        ready = []
        for pieces, turns in work:
            key_parts, value_parts = [], []
            for role, index in pieces:
                blocks = []
                for block, line in enumerate(line_of(role, index)):
                    spot = jnp.broadcast_to(line, (CLASSES, BLK))
                    seen = (spot >= class_from) & (spot <= class_to)
                    extra = jnp.where(seen, 0.0, MASKED).astype(jnp.bfloat16)
                    blocks.append(
                        jnp.concatenate([held[role, index, block * BLK : (block + 1) * BLK, :], extra], axis=0)
                    )
                key_parts.append(jnp.concatenate(blocks, axis=1))
                value_parts.append(with_ones(held[role, index, KSEG:PIECE, :]))
            value_all = jnp.concatenate(value_parts, axis=0)
            for part_at in [2 * turn + half for turn in turns for half in range(2)]:
                rows = slice(part_at * ROWS, (part_at + 1) * ROWS)
                scores = []
                for key in key_parts:
                    score = exact(scaled[rows, 0 : HD + CLASSES], key)
                    scores += [score[:, 0:BLK], score[:, BLK : 2 * BLK]]
                ready.append((rows, scores, value_all))
        for rows, scores, value_all in ready:
            largest = functools.reduce(jnp.maximum, scores)
            old = top[rows, :]
            new = jnp.maximum(old, jnp.max(largest, axis=1, keepdims=True))
            top[rows, :] = new
            factor = jnp.exp2((old - new) * SCALE)
            expo = jnp.concatenate(
                [jnp.exp2((score - new) * SCALE).astype(jnp.bfloat16) for score in scores], axis=1
            )
            added = exact(expo, value_all)
            total[rows, 0:HD] = total[rows, 0:HD] * factor + added[:, 0:HD]
            total[rows, HD : 2 * HD] = total[rows, HD : 2 * HD] * factor + added[:, HD : 2 * HD]

    def block_core(at):
        return jnp.where((at % 16) // 8 == 0, core, other)

    came = iota((BLK, MIXED), 1)
    expand = one_hot(iota((BLK, MIXED), 0) == 2 * (2 * (came // 16) + block_core(came)) + core)
    owner_rows = jnp.broadcast_to(owner[...].astype(jnp.float32), (8, BLK)).astype(jnp.bfloat16)
    owner_of = exact(owner_rows, expand)[0:1, :].astype(jnp.int32)
    code_in = owner_of * 8 + iota((1, MIXED), 1) % 8
    leaves = iota((MIXED, BLK), 0)
    code_out = (2 * (leaves // 16) + block_core(leaves)) * 8 + leaves % 8
    for at in range(MIXED // BLK):
        columns = slice(at * BLK, (at + 1) * BLK)
        mix[:, columns] = one_hot(code_out == jnp.broadcast_to(code_in[:, columns], (MIXED, BLK)))

    at_out, at_in = iota((ROWS, ROWS), 0), iota((ROWS, ROWS), 1)
    shuffle[0] = one_hot(at_in == (at_out % 8) * TURN + at_out // 8)
    shuffle[1] = one_hot(at_in == (at_out % TURN) * 8 + ((at_out % 64) // TURN) * GROUP + at_out // 64)

    start = (2 * CHIPS - 1) % BATCH
    steps = (2 * CHIPS - 1) // BATCH
    reached = [min(CHIPS - 1, (start + BATCH * step) // 2 + LOOKAHEAD) for step in range(steps)] + [CHIPS - 1]

    def events(step, low, high):
        if high - low == 1:
            indices = tuple(range(reached[low] + 1, reached[low + 1] + 1))
            if indices:
                forward(indices)
            return
        middle = (low + high) // 2

        @pl.when(step < middle)
        def _():
            events(step, low, middle)

        @pl.when(step >= middle)
        def _():
            events(step, middle, high)

    def used(at):
        own = at % 2
        return (core + 1 + own) % 2, (at + own) // 2

    def batch(step, get):
        return [get(start + BATCH * step + each) for each in range(BATCH)]

    def take(step):
        last = 2 * step + 3

        @pl.when(step < steps - 1)
        def _():
            pair_copy(other, last).wait_recv()

        @pl.when(step == steps - 1)
        def _():
            copy((other, CHIPS - 1), "all", 0, CHIPS - 1, me).wait_recv()

        return batch(step, used)

    forward(tuple(range(1, reached[0] + 1)))
    copy((other, 0), "all", 0, 0, me).wait_recv()
    pair_copy(other, 1).wait_recv()
    attend(([used(jnp.int32(at)) for at in range(start)], (0, 1)))

    def both_halves(step, carry):
        events(step, 0, steps)
        attend((take(step), (0, 1)))
        return carry

    lax.fori_loop(0, steps, both_halves, 0)

    def swap(turn, way):
        return pltpu.make_async_remote_copy(
            src_ref=swap_out.at[way, turn], dst_ref=swap_in.at[way, turn],
            send_sem=swap_send.at[way, turn], recv_sem=swap_recv.at[way, turn],
            device_id=sibling, device_id_type=MESH,
        )

    def spread(turn, way):
        target = spread_in if way == 0 else back_in

        def one(step, carry):
            there = ctx_of((place.x + step // NZ) % NX, (place.z + step % NZ) % NZ, core)
            pltpu.make_async_remote_copy(
                src_ref=spread_out.at[way, turn, there // CORES], dst_ref=target.at[turn, place.chip_here],
                send_sem=spread_send.at[way, turn], recv_sem=spread_recv.at[way, turn],
                device_id=place.device(there), device_id_type=MESH,
            ).start()
            return carry

        lax.fori_loop(1, CHIPS, one, 0)
        target[turn, place.chip_here] = spread_out[way, turn, place.chip_here]

    def spread_arrived(turn, way):
        target = spread_in if way == 0 else back_in
        many = target.at[turn, pl.ds(0, CHIPS - 1)]
        pltpu.make_async_copy(many, many, spread_recv.at[way, turn]).wait()

    def spread_sent(turn, way):
        many = spread_out.at[way, turn, pl.ds(0, CHIPS - 1)]
        pltpu.make_async_copy(many, many, spread_send.at[way, turn]).wait()

    def close(turn):
        done = [
            (total[rows, 0:HD] / total[rows, HD : 2 * HD]).astype(jnp.bfloat16)
            for rows in (rows_of(turn, head) for head in range(GROUP))
        ]
        for block in range(2):
            starts = [block * 2 * TURN + side * TURN for side in range(2)]
            planes = [done[head][start : start + TURN, :] for start in starts for head in range(GROUP)]
            owned[turn, block] = exact(shuffle[0], jnp.concatenate(planes, axis=0)).astype(jnp.bfloat16)
        swap_out[0, turn] = owned[turn, other]
        swap(turn, 0).start()

    def eights(rows):
        return rows.astype(jnp.float32).reshape(CHIPS, 8, HD)

    def deal(turn):
        swap(turn, 0).wait_recv()
        both = jnp.concatenate([eights(owned[turn, core]), eights(swap_in[0, turn])], axis=1)
        spread_out[0, turn] = both.astype(jnp.bfloat16)
        spread(turn, 0)

    def reorder(turn):
        spread_arrived(turn, 0)
        came_rows = spread_in[turn].reshape(MIXED, HD)
        spread_out[1, turn] = exact(mix[...], came_rows).astype(jnp.bfloat16).reshape(CHIPS, 16, HD)
        spread(turn, 1)

    def collect(turn):
        spread_arrived(turn, 1)
        landed = back_in[turn].astype(jnp.float32)
        owned[turn, core] = landed[:, 0:8, :].reshape(ROWS, HD).astype(jnp.bfloat16)
        swap_out[1, turn] = landed[:, 8:16, :].reshape(ROWS, HD).astype(jnp.bfloat16)
        swap(turn, 1).start()

    def give(turn, message):
        way = 1 if message % 2 == 0 else -1
        side = (0, 1, 1, 0, 0, 1)[message]
        dest = place.plane(2 if message < 2 else way)
        if message < 2:
            target = first_in.at[turn, message]
        else:
            target = last_in.at[turn, message % 2, side]
        return pltpu.make_async_remote_copy(
            src_ref=part.at[turn, dest, side], dst_ref=target,
            send_sem=sum_send.at[turn, message], recv_sem=sum_recv.at[turn, message],
            device_id={"ctx": me, "head": place.plane(way)}, device_id_type=MESH,
        )

    def project(turn):
        swap(turn, 1).wait_recv()
        owned[turn, other] = swap_in[1, turn]
        lefts = []
        for block in range(2):
            sorted_rows = exact(shuffle[1], owned[turn, block]).astype(jnp.bfloat16)
            lefts.append(jnp.concatenate([sorted_rows[64 * head : 64 * (head + 1), :] for head in range(GROUP)], axis=1))
        left = jnp.concatenate(lefts, axis=0)
        for side in range(2):
            for at in range(2):
                start = side * HALF + at * (HALF // 2)
                product = exact(left, proj[:, start : start + HALF // 2]).astype(jnp.bfloat16)
                for dest in range(HEADS):
                    part[turn, dest, side, :, at * (HALF // 2) : (at + 1) * (HALF // 2)] = product[
                        dest * TURN : (dest + 1) * TURN, :
                    ]
        for message in range(4):
            give(turn, message).start()
    def relay(turn):
        for message in (4, 5):
            way = 1 if message == 4 else -1
            side = message - 4
            give(turn, message - 4).wait_recv()
            dest = place.plane(way)
            merged = part[turn, dest, side].astype(jnp.float32) + first_in[turn, side].astype(jnp.float32)
            part[turn, dest, side] = merged.astype(jnp.bfloat16)
            give(turn, message).start()

    def finish(turn):
        for message in range(2, 6):
            give(turn, message).wait_recv()
        for side in range(2):
            summed = part[turn, place.head, side].astype(jnp.float32)
            for way in range(2):
                summed = summed + last_in[turn, way, side].astype(jnp.float32)
            out[turn * TURN : (turn + 1) * TURN, side * HALF : (side + 1) * HALF] = summed.astype(jnp.bfloat16)

    close(0)
    close(1)
    deal(0)
    deal(1)
    reorder(0)
    loads[6].wait()
    collect(0)
    project(0)
    reorder(1)
    relay(0)
    collect(1)
    project(1)
    relay(1)
    finish(0)

    for role in range(2):

        @pl.when(core == role)
        def _(role=role):
            for index in range(CHIPS):
                for each in sends(role, index):
                    each.wait_send()

    finish(1)

    for turn in range(2):
        for way in range(2):
            swap(turn, way).wait_send()
            spread_sent(turn, way)
        for message in range(6):
            give(turn, message).wait_send()


def local(queries, keys, values, segments, block_ranges, owner, out_proj):
    anywhere = pl.BlockSpec(memory_space=pltpu.HBM)
    bf16, i32, f32 = jnp.bfloat16, jnp.int32, jnp.float32
    dma = pltpu.SemaphoreType.DMA
    return pl.pallas_call(
        kernel,
        out_shape=jax.ShapeDtypeStruct((ROWS // HEADS, WIDE), bf16),
        in_specs=[anywhere] * 7,
        out_specs=pl.BlockSpec(memory_space=pltpu.VMEM),
        scratch_shapes=[
            pltpu.VMEM((ROWS, GROUP * HD), bf16),
            pltpu.VMEM((ROWS, HD), bf16),
            pltpu.VMEM((2, BLK), i32),
            pltpu.VMEM((3, 2 * CTX), i32),
            pltpu.VMEM((1, 2 * CTX), i32),
            pltpu.VMEM((GROUP * HD, WIDE), bf16),
            dma((7,)),
            pltpu.VMEM((2, CHIPS, PIECE, HD), bf16),
            pltpu.VMEM((GROUP * ROWS, 2 * HD), bf16),
            pltpu.VMEM((GROUP * ROWS, 2 * HD), f32),
            pltpu.VMEM((GROUP * ROWS, HD), f32),
            dma((2, CHIPS, 2)),
            dma((CHIPS, 5)),
            pltpu.VMEM((2, ROWS, ROWS), bf16),
            pltpu.VMEM((2, 2, ROWS, HD), bf16),
            pltpu.VMEM((2, 2, ROWS, HD), bf16),
            pltpu.VMEM((2, 2, CHIPS, 16, HD), bf16),
            pltpu.VMEM((2, CHIPS, 16, HD), bf16),
            pltpu.VMEM((2, CHIPS, 16, HD), bf16),
            pltpu.VMEM((MIXED, MIXED), bf16),
            pltpu.VMEM((2, 2, ROWS, HD), bf16),
            dma((2, 2)),
            dma((2, 2)),
            dma((2, 2)),
            dma((2, 2)),
            pltpu.VMEM((2, HEADS, 2, TURN, HALF), bf16),
            pltpu.VMEM((2, 2, TURN, HALF), bf16),
            pltpu.VMEM((2, 2, 2, TURN, HALF), bf16),
            dma((2, 6)),
            dma((2, 6)),
        ],
        compiler_params=pltpu.CompilerParams(
            collective_id=0, has_side_effects=True, vmem_limit_bytes=60 << 20
        ),
        cost_estimate=pl.CostEstimate(
            flops=4 * GROUP * ROWS * ROWS * CTX * HD,
            bytes_accessed=GROUP * HD * WIDE * 2,
            transcendentals=GROUP * ROWS * ROWS * CTX,
        ),
        name="attend_and_project",
    )(
        queries, keys, values, segments.reshape(2, BLK), block_ranges.T, owner.reshape(1, 2 * CTX), out_proj
    )


def solution(mesh):
    return jax.shard_map(
        local,
        mesh=mesh,
        in_specs=(
            P("ctx", "head"),
            P("ctx", "head"),
            P("ctx", "head"),
            P("ctx"),
            P(),
            P(),
            P("head", None),
        ),
        out_specs=P(("ctx", "head"), None),
        check_vma=False,
    )
```

```python
import functools
import math

import jax
import jax.numpy as jnp
from jax import lax
from jax.experimental import pallas as pl
from jax.experimental.pallas import tpu as pltpu
from jax.sharding import PartitionSpec as P

MESH = pl.DeviceIdType.MESH
HD = 128
BLK = 128
GROUP = 4
NX, NZ, CORES = 4, 8, 2
CTX = NX * NZ * CORES
HEADS = 4
ROWS = 256
KSEG = ROWS + 16
PIECE = KSEG + ROWS
CHIPS = NX * NZ
WIDE = 4096
HALF = WIDE // 2
TURN = 32
MIXED = CHIPS * 16
CLASSES = 16
BATCH = 4
LOOKAHEAD = 3
DOC_STEP = 32768
MASKED = -1e30
SCALE = math.log2(math.e) / math.sqrt(HD)


def ctx_of(x, z, core):
    return (x * NZ + z) * CORES + core


def ring_offsets(size):
    half = size // 2
    found = [0]
    for step in range(1, half):
        found += [step, -step]
    return found + [half]


def piece_order(size_a, size_b):
    pieces = [(da, db) for da in ring_offsets(size_a) for db in ring_offsets(size_b)]
    weights = [2 if size == NX else 3 for size in (size_a, size_b)]
    return sorted(pieces, key=lambda piece: weights[0] * abs(piece[0]) + weights[1] * abs(piece[1]))


ORDERS = (piece_order(NX, NZ), piece_order(NZ, NX))


class Place:
    def __init__(self):
        ctx = lax.axis_index("ctx")
        self.ctx = ctx
        self.head = lax.axis_index("head")
        self.core = ctx % CORES
        self.z = (ctx // CORES) % NZ
        self.x = ctx // (CORES * NZ)
        self.chip_here = ctx // CORES

    def chip(self, dx, dz, core):
        return ctx_of((self.x + dx + NX) % NX, (self.z + dz + NZ) % NZ, core)

    def device(self, ctx):
        return {"ctx": ctx, "head": self.head}

    def plane(self, step):
        return (self.head + step) % HEADS


def iota(shape, dim):
    return lax.broadcasted_iota(jnp.int32, shape, dim)


def one_hot(mask):
    return jnp.where(mask, 1.0, 0.0).astype(jnp.bfloat16)


def exact(left, right):
    return jnp.dot(left, right, preferred_element_type=jnp.float32)


def kernel(
    queries_hbm, keys_hbm, values_hbm, segs_hbm, ranges_hbm, owner_hbm, proj_hbm, out,
    queries, keys, segs, ranges, owner, proj, load_sem,
    held, scaled, total, top, recv_sem, send_sem,
    shuffle, swap_out, swap_in, spread_out, spread_in, back_in, mix, owned, swap_send, swap_recv, spread_send, spread_recv,
    part, first_in, last_in, sum_send, sum_recv,
    tiles_out, tiles_in, tiles_back, tiles_send, tiles_recv,
):
    place = Place()
    me, core, other = place.ctx, place.core, 1 - place.core

    loads = [
        pltpu.make_async_copy(source, target, load_sem.at[at])
        for at, (source, target) in enumerate(
            (
                (keys_hbm, keys),
                (segs_hbm, segs),
                (values_hbm, held.at[core, 0, pl.ds(KSEG, ROWS), :]),
                (queries_hbm, queries),
                (ranges_hbm, ranges),
                (owner_hbm, owner),
                (proj_hbm, proj),
            )
        )
    ]
    for load in loads:
        load.start()

    barrier = pltpu.get_barrier_semaphore()
    sibling = place.device(place.chip(0, 0, other))

    around = [place.device(place.chip(dx, dz, core)) for dx, dz in ((1, 0), (-1, 0), (0, 1), (0, -1))]
    around += [sibling] + [{"ctx": me, "head": place.plane(step)} for step in (1, -1)]
    for device in around:
        pl.semaphore_signal(barrier, inc=1, device_id=device, device_id_type=MESH)

    for load in loads[:3]:
        load.wait()
    for block in range(2):
        turned = jnp.transpose(keys[block * BLK : (block + 1) * BLK, :].astype(jnp.float32))
        held[core, 0, block * BLK : (block + 1) * BLK, :] = turned.astype(jnp.bfloat16)
    seg_rows = segs[...].astype(jnp.float32)
    held[core, 0, ROWS:KSEG, :] = jnp.concatenate(
        [seg_rows, jnp.full((1, BLK), me, jnp.int32).astype(jnp.float32), jnp.zeros((13, BLK), jnp.float32)], axis=0
    ).astype(jnp.bfloat16)
    pl.semaphore_wait(barrier, len(around))

    parts = {"all": (0, PIECE, 0), "keys": (0, KSEG, 0), "values": (KSEG, ROWS, 1)}

    def copy(piece, name, kind, at, device):
        role, index = piece
        start, size, which = parts[name]
        return pltpu.make_async_remote_copy(
            src_ref=held.at[role, index, pl.ds(start, size), :],
            dst_ref=held.at[role, at, pl.ds(start, size), :],
            send_sem=send_sem.at[index, kind], recv_sem=recv_sem.at[role, at, which],
            device_id=place.device(device), device_id_type=MESH,
        )

    def pair_copy(role, index):
        pair = held.at[role, pl.ds(index, 2)]
        return pltpu.make_async_remote_copy(
            src_ref=pair, dst_ref=pair, send_sem=send_sem.at[index, 4], recv_sem=recv_sem.at[role, index, 0],
            device_id=sibling, device_id_type=MESH,
        )

    def sends(role, index):
        order = ORDERS[role]
        sizes = (NX, NZ) if role == 0 else (NZ, NX)
        offsets = order[index]
        found = []

        def go(name, axis, way):
            moved = list(offsets)
            moved[axis] -= way
            for each in range(2):
                if moved[each] <= -sizes[each] // 2:
                    moved[each] += sizes[each]
            step = [0, 0]
            step[axis] = way
            dx, dz = step if role == 0 else step[::-1]
            kind = 2 * axis + (0 if way > 0 else 1)
            found.append(copy((role, index), name, kind, order.index(tuple(moved)), place.chip(dx, dz, role)))

        for axis in range(2):
            if axis == 0 and offsets[1] != 0:
                continue
            offset, half = offsets[axis], sizes[axis] // 2
            if offset == 0:
                go("all", axis, 1)
                go("all", axis, -1)
            elif abs(offset) < half:
                name = "all" if abs(offset) < half - 1 else ("keys" if offset > 0 else "values")
                go(name, axis, -1 if offset > 0 else 1)
        if index in (0, CHIPS - 1):
            found.append(copy((role, index), "all", 4, index, place.chip(0, 0, 1 - role)))
        elif index % 2 == 0:
            found.append(pair_copy(role, index - 1))
        return found

    def arrive(role, index):
        da, db = ORDERS[role][index]
        sizes = (NX, NZ) if role == 0 else (NZ, NX)
        if index == 0:
            return
        halves = db == sizes[1] // 2 or (db == 0 and da == sizes[0] // 2)
        for name in ("keys", "values") if halves else ("all",):
            copy((role, index), name, 0, index, me).wait_recv()

    def forward(indices):
        for role in range(2):

            @pl.when(core == role)
            def _(role=role):
                for index in indices:
                    arrive(role, index)
                    for each in sends(role, index):
                        each.start()

    forward((0,))

    for load in loads[3:6]:
        load.wait()
    lane = iota((1, BLK), 1)
    bounds = []
    for block in range(2):
        picked = jnp.where(lane == 2 * me + block, ranges[...], 0).astype(jnp.float32)
        bounds.append(jnp.sum(picked, axis=1, keepdims=True).astype(jnp.int32))
    row = iota((CLASSES, BLK), 0)
    low, high = (
        jnp.where(
            row < 3,
            jnp.broadcast_to(bounds[0][at : at + 1, :], (CLASSES, BLK)),
            jnp.broadcast_to(bounds[1][at : at + 1, :], (CLASSES, BLK)),
        )
        for at in range(2)
    )
    class_seg = jnp.where(row < 3, row, row - 3) * DOC_STEP
    class_from = low * BLK + class_seg
    class_to = high * BLK + (BLK - 1) + class_seg

    row_seg = [
        jnp.transpose(jnp.broadcast_to(seg_rows[block : block + 1, :], (BLK, BLK))).astype(jnp.int32)
        for block in range(2)
    ]
    row_class = jnp.concatenate([row_seg[0], row_seg[1] + 3], axis=0)
    chosen = one_hot(row_class[:, 0:CLASSES] == iota((ROWS, CLASSES), 1))
    def by_turn(array, turn):
        starts = [block * BLK + side * 2 * TURN + turn * TURN for block in range(2) for side in range(2)]
        return jnp.concatenate([array[start : start + TURN, :] for start in starts], axis=0)

    def rows_of(turn, head):
        start = turn * GROUP * BLK + head * BLK
        return slice(start, start + BLK)

    all_queries = queries[...]
    for turn in range(2):
        turn_queries, turn_chosen = by_turn(all_queries, turn), by_turn(chosen, turn)
        for head in range(GROUP):
            scaled[rows_of(turn, head), 0:HD] = turn_queries[:, head * HD : (head + 1) * HD]
            scaled[rows_of(turn, head), HD : HD + CLASSES] = turn_chosen

    def with_ones(value):
        return jnp.concatenate([value, jnp.ones_like(value)], axis=1)

    def line_of(role, index):
        info = held[role, index, ROWS:KSEG, :].astype(jnp.float32).astype(jnp.int32)
        base = info[2:3, :] * ROWS + lane
        return [info[block : block + 1, :] * DOC_STEP + base + block * BLK for block in range(2)]

    own_key = jnp.concatenate([held[core, 0, 0:BLK, :], held[core, 0, BLK : 2 * BLK, :]], axis=1)
    own_value = with_ones(held[core, 0, KSEG:PIECE, :])
    own_line = jnp.concatenate(line_of(core, 0), axis=1)
    inside = []
    for block in range(2):
        low, high, causal = (jnp.broadcast_to(bounds[block][i : i + 1, :], (BLK, BLK)) for i in range(3))
        pos = me * ROWS + block * BLK + iota((BLK, BLK), 0)
        end = high * BLK + (BLK - 1)
        end = jnp.where(causal == 0, end, jnp.minimum(end, pos)) + row_seg[block] * DOC_STEP
        start = low * BLK + row_seg[block] * DOC_STEP
        wide = jnp.broadcast_to(own_line, (BLK, ROWS))
        inside.append(
            (wide >= jnp.concatenate([start, start], axis=1)) & (wide <= jnp.concatenate([end, end], axis=1))
        )
    hidden = jnp.where(jnp.concatenate(inside, axis=0), 0.0, MASKED)
    for part_at in range(GROUP):
        rows = slice(part_at * ROWS, (part_at + 1) * ROWS)
        turn_hidden = by_turn(hidden, part_at // 2)
        score = exact(scaled[rows, 0:HD], own_key)
        score = jnp.where(jnp.concatenate([turn_hidden, turn_hidden], axis=0) < 0.0, MASKED, score)
        new = jnp.broadcast_to(jnp.max(score, axis=1, keepdims=True), (ROWS, HD))
        top[rows, :] = new
        expo = jnp.concatenate(
            [jnp.exp2((score[:, at * BLK : (at + 1) * BLK] - new) * SCALE).astype(jnp.bfloat16) for at in range(2)],
            axis=1,
        )
        total[rows, :] = exact(expo, own_value)

    def attend(*work):
        ready = []
        for pieces, turns in work:
            key_parts, value_parts = [], []
            for role, index in pieces:
                blocks = []
                for block, line in enumerate(line_of(role, index)):
                    spot = jnp.broadcast_to(line, (CLASSES, BLK))
                    seen = (spot >= class_from) & (spot <= class_to)
                    extra = jnp.where(seen, 0.0, MASKED).astype(jnp.bfloat16)
                    blocks.append(
                        jnp.concatenate([held[role, index, block * BLK : (block + 1) * BLK, :], extra], axis=0)
                    )
                key_parts.append(jnp.concatenate(blocks, axis=1))
                value_parts.append(with_ones(held[role, index, KSEG:PIECE, :]))
            value_all = jnp.concatenate(value_parts, axis=0)
            for part_at in [2 * turn + half for turn in turns for half in range(2)]:
                rows = slice(part_at * ROWS, (part_at + 1) * ROWS)
                scores = []
                for key in key_parts:
                    score = exact(scaled[rows, 0 : HD + CLASSES], key)
                    scores += [score[:, 0:BLK], score[:, BLK : 2 * BLK]]
                ready.append((rows, scores, value_all))
        for rows, scores, value_all in ready:
            largest = functools.reduce(jnp.maximum, scores)
            old = top[rows, :]
            new = jnp.maximum(old, jnp.max(largest, axis=1, keepdims=True))
            top[rows, :] = new
            factor = jnp.exp2((old - new) * SCALE)
            expo = jnp.concatenate(
                [jnp.exp2((score - new) * SCALE).astype(jnp.bfloat16) for score in scores], axis=1
            )
            added = exact(expo, value_all)
            total[rows, 0:HD] = total[rows, 0:HD] * factor + added[:, 0:HD]
            total[rows, HD : 2 * HD] = total[rows, HD : 2 * HD] * factor + added[:, HD : 2 * HD]

    def block_core(at):
        return jnp.where((at % 16) // 8 == 0, core, other)

    came = iota((BLK, MIXED), 1)
    expand = one_hot(iota((BLK, MIXED), 0) == 2 * (2 * (came // 16) + block_core(came)) + core)
    owner_rows = jnp.broadcast_to(owner[...].astype(jnp.float32), (8, BLK)).astype(jnp.bfloat16)
    owner_of = exact(owner_rows, expand)[0:1, :].astype(jnp.int32)
    code_in = owner_of * 8 + iota((1, MIXED), 1) % 8
    leaves = iota((MIXED, BLK), 0)
    code_out = (2 * (leaves // 16) + block_core(leaves)) * 8 + leaves % 8
    for at in range(MIXED // BLK):
        columns = slice(at * BLK, (at + 1) * BLK)
        mix[:, columns] = one_hot(code_out == jnp.broadcast_to(code_in[:, columns], (MIXED, BLK)))

    at_out, at_in = iota((ROWS, ROWS), 0), iota((ROWS, ROWS), 1)
    shuffle[0] = one_hot(at_in == (at_out % 8) * TURN + at_out // 8)
    shuffle[1] = one_hot(at_in == (at_out % TURN) * 8 + ((at_out % 64) // TURN) * GROUP + at_out // 64)

    start = (2 * CHIPS - 1) % BATCH
    steps = (2 * CHIPS - 1) // BATCH
    reached = [min(CHIPS - 1, (start + BATCH * step) // 2 + LOOKAHEAD) for step in range(steps)] + [CHIPS - 1]

    def events(step, low, high):
        if high - low == 1:
            indices = tuple(range(reached[low] + 1, reached[low + 1] + 1))
            if indices:
                forward(indices)
            return
        middle = (low + high) // 2

        @pl.when(step < middle)
        def _():
            events(step, low, middle)

        @pl.when(step >= middle)
        def _():
            events(step, middle, high)

    def used(at):
        own = at % 2
        return (core + 1 + own) % 2, (at + own) // 2

    def batch(step, get):
        return [get(start + BATCH * step + each) for each in range(BATCH)]

    def take(step):
        last = 2 * step + 3

        @pl.when(step < steps - 1)
        def _():
            pair_copy(other, last).wait_recv()

        @pl.when(step == steps - 1)
        def _():
            copy((other, CHIPS - 1), "all", 0, CHIPS - 1, me).wait_recv()

        return batch(step, used)

    forward(tuple(range(1, reached[0] + 1)))
    copy((other, 0), "all", 0, 0, me).wait_recv()
    pair_copy(other, 1).wait_recv()
    attend(([used(jnp.int32(at)) for at in range(start)], (0, 1)))

    def both_halves(step, carry):
        events(step, 0, steps)
        attend((take(step), (0, 1)))
        return carry

    lax.fori_loop(0, steps, both_halves, 0)

    def swap(turn, way):
        return pltpu.make_async_remote_copy(
            src_ref=swap_out.at[way, turn], dst_ref=swap_in.at[way, turn],
            send_sem=swap_send.at[way, turn], recv_sem=swap_recv.at[way, turn],
            device_id=sibling, device_id_type=MESH,
        )

    def spread(turn, way):
        target = spread_in if way == 0 else back_in

        def one(step, carry):
            there = ctx_of((place.x + step // NZ) % NX, (place.z + step % NZ) % NZ, core)
            pltpu.make_async_remote_copy(
                src_ref=spread_out.at[way, turn, there // CORES], dst_ref=target.at[turn, place.chip_here],
                send_sem=spread_send.at[way, turn], recv_sem=spread_recv.at[way, turn],
                device_id=place.device(there), device_id_type=MESH,
            ).start()
            return carry

        lax.fori_loop(1, CHIPS, one, 0)
        target[turn, place.chip_here] = spread_out[way, turn, place.chip_here]

    def spread_arrived(turn, way):
        target = spread_in if way == 0 else back_in
        many = target.at[turn, pl.ds(0, CHIPS - 1)]
        pltpu.make_async_copy(many, many, spread_recv.at[way, turn]).wait()

    def spread_sent(turn, way):
        many = spread_out.at[way, turn, pl.ds(0, CHIPS - 1)]
        pltpu.make_async_copy(many, many, spread_send.at[way, turn]).wait()

    def attended(turn):
        return [
            (total[rows, 0:HD] / total[rows, HD : 2 * HD]).astype(jnp.bfloat16)
            for rows in (rows_of(turn, head) for head in range(GROUP))
        ]

    def close(turn):
        done = attended(turn)
        for block in range(2):
            starts = [block * 2 * TURN + side * TURN for side in range(2)]
            planes = [done[head][start : start + TURN, :] for start in starts for head in range(GROUP)]
            owned[turn, block] = exact(shuffle[0], jnp.concatenate(planes, axis=0)).astype(jnp.bfloat16)
        swap_out[0, turn] = owned[turn, other]
        swap(turn, 0).start()

    def eights(rows):
        return rows.astype(jnp.float32).reshape(CHIPS, 8, HD)

    def deal(turn):
        swap(turn, 0).wait_recv()
        both = jnp.concatenate([eights(owned[turn, core]), eights(swap_in[0, turn])], axis=1)
        spread_out[0, turn] = both.astype(jnp.bfloat16)
        spread(turn, 0)

    def reorder(turn):
        spread_arrived(turn, 0)
        came_rows = spread_in[turn].reshape(MIXED, HD)
        spread_out[1, turn] = exact(mix[...], came_rows).astype(jnp.bfloat16).reshape(CHIPS, 16, HD)
        spread(turn, 1)

    def collect(turn):
        spread_arrived(turn, 1)
        landed = back_in[turn].astype(jnp.float32)
        owned[turn, core] = landed[:, 0:8, :].reshape(ROWS, HD).astype(jnp.bfloat16)
        swap_out[1, turn] = landed[:, 8:16, :].reshape(ROWS, HD).astype(jnp.bfloat16)
        swap(turn, 1).start()

    def give(turn, message):
        way = 1 if message % 2 == 0 else -1
        side = (0, 1, 1, 0, 0, 1)[message]
        dest = place.plane(2 if message < 2 else way)
        if message < 2:
            target = first_in.at[turn, message]
        else:
            target = last_in.at[turn, message % 2, side]
        return pltpu.make_async_remote_copy(
            src_ref=part.at[turn, dest, side], dst_ref=target,
            send_sem=sum_send.at[turn, message], recv_sem=sum_recv.at[turn, message],
            device_id={"ctx": me, "head": place.plane(way)}, device_id_type=MESH,
        )

    def owned_rows(turn):
        swap(turn, 1).wait_recv()
        owned[turn, other] = swap_in[1, turn]
        lefts = []
        for block in range(2):
            sorted_rows = exact(shuffle[1], owned[turn, block]).astype(jnp.bfloat16)
            lefts.append(jnp.concatenate([sorted_rows[64 * head : 64 * (head + 1), :] for head in range(GROUP)], axis=1))
        return jnp.concatenate(lefts, axis=0)

    def project(turn, left):
        for side in range(2):
            for at in range(2):
                start = side * HALF + at * (HALF // 2)
                product = exact(left, proj[:, start : start + HALF // 2]).astype(jnp.bfloat16)
                for dest in range(HEADS):
                    part[turn, dest, side, :, at * (HALF // 2) : (at + 1) * (HALF // 2)] = product[
                        dest * TURN : (dest + 1) * TURN, :
                    ]
        for message in range(4):
            give(turn, message).start()
    def relay(turn):
        for message in (4, 5):
            way = 1 if message == 4 else -1
            side = message - 4
            give(turn, message - 4).wait_recv()
            dest = place.plane(way)
            merged = part[turn, dest, side].astype(jnp.float32) + first_in[turn, side].astype(jnp.float32)
            part[turn, dest, side] = merged.astype(jnp.bfloat16)
            give(turn, message).start()

    def finish(turn):
        for message in range(2, 6):
            give(turn, message).wait_recv()
        for side in range(2):
            summed = part[turn, place.head, side].astype(jnp.float32)
            for way in range(2):
                summed = summed + last_in[turn, way, side].astype(jnp.float32)
            summed = summed.astype(jnp.bfloat16)
            if turn == 0:
                out[0:TURN, side * HALF : (side + 1) * HALF] = summed
                continue
            for at in range(HALF // HD):
                tiles_out[0, side * (HALF // HD) + at] = summed[:, at * HD : (at + 1) * HD]

    def tile_spread(way):
        target = tiles_in.at[0] if way == 0 else tiles_back

        def one(step, carry):
            there = ctx_of((place.x + step // NZ) % NX, (place.z + step % NZ) % NZ, core)
            pltpu.make_async_remote_copy(
                src_ref=tiles_out.at[way, there // CORES], dst_ref=target.at[place.chip_here],
                send_sem=tiles_send.at[way], recv_sem=tiles_recv.at[way],
                device_id=place.device(there), device_id_type=MESH,
            ).start()
            return carry

        lax.fori_loop(1, CHIPS, one, 0)
        target[place.chip_here] = tiles_out[way, place.chip_here]

    def tiles_wait(sem):
        many = tiles_back.at[pl.ds(0, CHIPS - 1)]
        pltpu.make_async_copy(many, many, sem).wait()

    tile_swap = pltpu.make_async_remote_copy(
        src_ref=tiles_in.at[0], dst_ref=tiles_in.at[1], send_sem=tiles_send.at[2], recv_sem=tiles_recv.at[2],
        device_id=sibling, device_id_type=MESH,
    )

    def tiles_choose():
        tile_swap.wait_recv()
        for chip in range(CHIPS):
            mine = (owner[...] == CORES * chip + core) & (lane % 2 == place.head // 2)
            home = jnp.clip(jnp.sum(jnp.where(mine, lane, 0)) // 2, 0, CTX - 1)
            tiles_out[1, chip] = tiles_in[(home + core) % 2, home // 2]

    loads[6].wait()
    project(1, jnp.concatenate(attended(1), axis=1))
    close(0)
    deal(0)
    relay(1)
    reorder(0)
    collect(0)
    finish(1)
    tile_spread(0)
    project(0, owned_rows(0))
    relay(0)
    tiles_wait(tiles_recv.at[0])
    tile_swap.start()
    tiles_choose()
    tile_spread(1)
    for role in range(2):

        @pl.when(core == role)
        def _(role=role):
            for index in range(CHIPS):
                for each in sends(role, index):
                    each.wait_send()

    finish(0)
    tiles_wait(tiles_recv.at[1])
    for at in range(CHIPS):
        out[TURN : 2 * TURN, at * HD : (at + 1) * HD] = tiles_back[at]

    for way in range(2):
        swap(0, way).wait_send()
        spread_sent(0, way)
        tiles_wait(tiles_send.at[way])
    tile_swap.wait_send()
    for turn in range(2):
        for message in range(6):
            give(turn, message).wait_send()


def local(queries, keys, values, segments, block_ranges, owner, out_proj):
    anywhere = pl.BlockSpec(memory_space=pltpu.HBM)
    bf16, i32, f32 = jnp.bfloat16, jnp.int32, jnp.float32
    dma = pltpu.SemaphoreType.DMA
    return pl.pallas_call(
        kernel,
        out_shape=jax.ShapeDtypeStruct((ROWS // HEADS, WIDE), bf16),
        in_specs=[anywhere] * 7,
        out_specs=pl.BlockSpec(memory_space=pltpu.VMEM),
        scratch_shapes=[
            pltpu.VMEM((ROWS, GROUP * HD), bf16),
            pltpu.VMEM((ROWS, HD), bf16),
            pltpu.VMEM((2, BLK), i32),
            pltpu.VMEM((3, 2 * CTX), i32),
            pltpu.VMEM((1, 2 * CTX), i32),
            pltpu.VMEM((GROUP * HD, WIDE), bf16),
            dma((7,)),
            pltpu.VMEM((2, CHIPS, PIECE, HD), bf16),
            pltpu.VMEM((GROUP * ROWS, 2 * HD), bf16),
            pltpu.VMEM((GROUP * ROWS, 2 * HD), f32),
            pltpu.VMEM((GROUP * ROWS, HD), f32),
            dma((2, CHIPS, 2)),
            dma((CHIPS, 5)),
            pltpu.VMEM((2, ROWS, ROWS), bf16),
            pltpu.VMEM((2, 2, ROWS, HD), bf16),
            pltpu.VMEM((2, 2, ROWS, HD), bf16),
            pltpu.VMEM((2, 2, CHIPS, 16, HD), bf16),
            pltpu.VMEM((2, CHIPS, 16, HD), bf16),
            pltpu.VMEM((2, CHIPS, 16, HD), bf16),
            pltpu.VMEM((MIXED, MIXED), bf16),
            pltpu.VMEM((2, 2, ROWS, HD), bf16),
            dma((2, 2)),
            dma((2, 2)),
            dma((2, 2)),
            dma((2, 2)),
            pltpu.VMEM((2, HEADS, 2, TURN, HALF), bf16),
            pltpu.VMEM((2, 2, TURN, HALF), bf16),
            pltpu.VMEM((2, 2, 2, TURN, HALF), bf16),
            dma((2, 6)),
            dma((2, 6)),
            pltpu.VMEM((2, CHIPS, TURN, HD), bf16),
            pltpu.VMEM((2, CHIPS, TURN, HD), bf16),
            pltpu.VMEM((CHIPS, TURN, HD), bf16),
            dma((3,)),
            dma((3,)),
        ],
        compiler_params=pltpu.CompilerParams(
            collective_id=0, has_side_effects=True, vmem_limit_bytes=60 << 20
        ),
        cost_estimate=pl.CostEstimate(
            flops=4 * GROUP * ROWS * ROWS * CTX * HD,
            bytes_accessed=GROUP * HD * WIDE * 2,
            transcendentals=GROUP * ROWS * ROWS * CTX,
        ),
        name="attend_and_project",
    )(
        queries, keys, values, segments.reshape(2, BLK), block_ranges.T, owner.reshape(1, 2 * CTX), out_proj
    )


def solution(mesh):
    return jax.shard_map(
        local,
        mesh=mesh,
        in_specs=(
            P("ctx", "head"),
            P("ctx", "head"),
            P("ctx", "head"),
            P("ctx"),
            P(),
            P(),
            P("head", None),
        ),
        out_specs=P(("ctx", "head"), None),
        check_vma=False,
    )
```

```python
import functools
import math

import jax
import jax.numpy as jnp
from jax import lax
from jax.experimental import pallas as pl
from jax.experimental.pallas import tpu as pltpu
from jax.sharding import PartitionSpec as P

MESH = pl.DeviceIdType.MESH
HD = 128
BLK = 128
GROUP = 4
NX, NZ, CORES = 4, 8, 2
CTX = NX * NZ * CORES
HEADS = 4
ROWS = 256
KSEG = ROWS + 16
PIECE = KSEG + ROWS
CHIPS = NX * NZ
WIDE = 4096
HALF = WIDE // 2
TURN = 32
MIXED = CHIPS * 16
CLASSES = 16
BATCH = 4
LOOKAHEAD = 3
DOC_STEP = 32768
MASKED = -1e30
SCALE = math.log2(math.e) / math.sqrt(HD)


def ctx_of(x, z, core):
    return (x * NZ + z) * CORES + core


def ring_offsets(size):
    half = size // 2
    found = [0]
    for step in range(1, half):
        found += [step, -step]
    return found + [half]


def piece_order(size_a, size_b):
    pieces = [(da, db) for da in ring_offsets(size_a) for db in ring_offsets(size_b)]
    weights = [2 if size == NX else 3 for size in (size_a, size_b)]
    return sorted(pieces, key=lambda piece: weights[0] * abs(piece[0]) + weights[1] * abs(piece[1]))


ORDERS = (piece_order(NX, NZ), piece_order(NZ, NX))


class Place:
    def __init__(self):
        ctx = lax.axis_index("ctx")
        self.ctx = ctx
        self.head = lax.axis_index("head")
        self.core = ctx % CORES
        self.z = (ctx // CORES) % NZ
        self.x = ctx // (CORES * NZ)
        self.chip_here = ctx // CORES

    def chip(self, dx, dz, core):
        return ctx_of((self.x + dx + NX) % NX, (self.z + dz + NZ) % NZ, core)

    def device(self, ctx):
        return {"ctx": ctx, "head": self.head}

    def plane(self, step):
        return (self.head + step) % HEADS


def iota(shape, dim):
    return lax.broadcasted_iota(jnp.int32, shape, dim)


def one_hot(mask):
    return jnp.where(mask, 1.0, 0.0).astype(jnp.bfloat16)


def exact(left, right):
    return jnp.dot(left, right, preferred_element_type=jnp.float32)


def kernel(
    queries_hbm, keys_hbm, values_hbm, segs_hbm, ranges_hbm, owner_hbm, proj_hbm, out,
    queries, keys, segs, ranges, owner, proj, load_sem,
    held, scaled, total, top, recv_sem, send_sem,
    shuffle, swap_out, swap_in, spread_out, spread_in, back_in, mix, owned, swap_send, swap_recv, spread_send, spread_recv,
    part, first_in, last_in, sum_send, sum_recv,
    tiles_out, tiles_in, tiles_back, tiles_send, tiles_recv,
):
    place = Place()
    me, core, other = place.ctx, place.core, 1 - place.core

    loads = [
        pltpu.make_async_copy(source, target, load_sem.at[at])
        for at, (source, target) in enumerate(
            (
                (keys_hbm, keys),
                (segs_hbm, segs),
                (values_hbm, held.at[core, 0, pl.ds(KSEG, ROWS), :]),
                (queries_hbm, queries),
                (ranges_hbm, ranges),
                (owner_hbm, owner),
                (proj_hbm, proj),
            )
        )
    ]
    for load in loads:
        load.start()

    barrier = pltpu.get_barrier_semaphore()
    sibling = place.device(place.chip(0, 0, other))

    around = [place.device(place.chip(dx, dz, core)) for dx, dz in ((1, 0), (-1, 0), (0, 1), (0, -1))]
    around += [sibling] + [{"ctx": me, "head": place.plane(step)} for step in (1, -1)]
    for device in around:
        pl.semaphore_signal(barrier, inc=1, device_id=device, device_id_type=MESH)

    for load in loads[:3]:
        load.wait()
    for block in range(2):
        turned = jnp.transpose(keys[block * BLK : (block + 1) * BLK, :].astype(jnp.float32))
        held[core, 0, block * BLK : (block + 1) * BLK, :] = turned.astype(jnp.bfloat16)
    seg_rows = segs[...].astype(jnp.float32)
    held[core, 0, ROWS:KSEG, :] = jnp.concatenate(
        [seg_rows, jnp.full((1, BLK), me, jnp.int32).astype(jnp.float32), jnp.zeros((13, BLK), jnp.float32)], axis=0
    ).astype(jnp.bfloat16)
    pl.semaphore_wait(barrier, len(around))

    parts = {"all": (0, PIECE, 0), "keys": (0, KSEG, 0), "values": (KSEG, ROWS, 1)}

    def copy(piece, name, kind, at, device):
        role, index = piece
        start, size, which = parts[name]
        return pltpu.make_async_remote_copy(
            src_ref=held.at[role, index, pl.ds(start, size), :],
            dst_ref=held.at[role, at, pl.ds(start, size), :],
            send_sem=send_sem.at[index, kind], recv_sem=recv_sem.at[role, at, which],
            device_id=place.device(device), device_id_type=MESH,
        )

    def pair_copy(role, index):
        pair = held.at[role, pl.ds(index, 2)]
        return pltpu.make_async_remote_copy(
            src_ref=pair, dst_ref=pair, send_sem=send_sem.at[index, 4], recv_sem=recv_sem.at[role, index, 0],
            device_id=sibling, device_id_type=MESH,
        )

    def sends(role, index):
        order = ORDERS[role]
        sizes = (NX, NZ) if role == 0 else (NZ, NX)
        offsets = order[index]
        found = []

        def go(name, axis, way):
            moved = list(offsets)
            moved[axis] -= way
            for each in range(2):
                if moved[each] <= -sizes[each] // 2:
                    moved[each] += sizes[each]
            step = [0, 0]
            step[axis] = way
            dx, dz = step if role == 0 else step[::-1]
            kind = 2 * axis + (0 if way > 0 else 1)
            found.append(copy((role, index), name, kind, order.index(tuple(moved)), place.chip(dx, dz, role)))

        for axis in range(2):
            if axis == 0 and offsets[1] != 0:
                continue
            offset, half = offsets[axis], sizes[axis] // 2
            if offset == 0:
                go("all", axis, 1)
                go("all", axis, -1)
            elif abs(offset) < half:
                name = "all" if abs(offset) < half - 1 else ("keys" if offset > 0 else "values")
                go(name, axis, -1 if offset > 0 else 1)
        if index in (0, CHIPS - 1):
            found.append(copy((role, index), "all", 4, index, place.chip(0, 0, 1 - role)))
        elif index % 2 == 0:
            found.append(pair_copy(role, index - 1))
        return found

    def arrive(role, index):
        da, db = ORDERS[role][index]
        sizes = (NX, NZ) if role == 0 else (NZ, NX)
        if index == 0:
            return
        halves = db == sizes[1] // 2 or (db == 0 and da == sizes[0] // 2)
        for name in ("keys", "values") if halves else ("all",):
            copy((role, index), name, 0, index, me).wait_recv()

    def forward(indices):
        for role in range(2):

            @pl.when(core == role)
            def _(role=role):
                for index in indices:
                    arrive(role, index)
                    for each in sends(role, index):
                        each.start()

    forward((0,))

    for load in loads[3:6]:
        load.wait()
    lane = iota((1, BLK), 1)
    bounds = []
    for block in range(2):
        picked = jnp.where(lane == 2 * me + block, ranges[...], 0).astype(jnp.float32)
        bounds.append(jnp.sum(picked, axis=1, keepdims=True).astype(jnp.int32))
    row = iota((CLASSES, BLK), 0)
    low, high = (
        jnp.where(
            row < 3,
            jnp.broadcast_to(bounds[0][at : at + 1, :], (CLASSES, BLK)),
            jnp.broadcast_to(bounds[1][at : at + 1, :], (CLASSES, BLK)),
        )
        for at in range(2)
    )
    class_seg = jnp.where(row < 3, row, row - 3) * DOC_STEP
    class_from = low * BLK + class_seg
    class_to = high * BLK + (BLK - 1) + class_seg

    row_seg = [
        jnp.transpose(jnp.broadcast_to(seg_rows[block : block + 1, :], (BLK, BLK))).astype(jnp.int32)
        for block in range(2)
    ]
    row_class = jnp.concatenate([row_seg[0], row_seg[1] + 3], axis=0)
    chosen = one_hot(row_class[:, 0:CLASSES] == iota((ROWS, CLASSES), 1))
    def by_turn(array, turn):
        starts = [block * BLK + side * 2 * TURN + turn * TURN for block in range(2) for side in range(2)]
        return jnp.concatenate([array[start : start + TURN, :] for start in starts], axis=0)

    def rows_of(turn, head):
        start = turn * GROUP * BLK + head * BLK
        return slice(start, start + BLK)

    all_queries = queries[...]
    for turn in range(2):
        turn_queries, turn_chosen = by_turn(all_queries, turn), by_turn(chosen, turn)
        for head in range(GROUP):
            scaled[rows_of(turn, head), 0:HD] = turn_queries[:, head * HD : (head + 1) * HD]
            scaled[rows_of(turn, head), HD : HD + CLASSES] = turn_chosen

    def with_ones(value):
        return jnp.concatenate([value, jnp.ones_like(value)], axis=1)

    def line_of(role, index):
        info = held[role, index, ROWS:KSEG, :].astype(jnp.float32).astype(jnp.int32)
        base = info[2:3, :] * ROWS + lane
        return [info[block : block + 1, :] * DOC_STEP + base + block * BLK for block in range(2)]

    own_key = jnp.concatenate([held[core, 0, 0:BLK, :], held[core, 0, BLK : 2 * BLK, :]], axis=1)
    own_value = with_ones(held[core, 0, KSEG:PIECE, :])
    own_line = jnp.concatenate(line_of(core, 0), axis=1)
    inside = []
    for block in range(2):
        low, high, causal = (jnp.broadcast_to(bounds[block][i : i + 1, :], (BLK, BLK)) for i in range(3))
        pos = me * ROWS + block * BLK + iota((BLK, BLK), 0)
        end = high * BLK + (BLK - 1)
        end = jnp.where(causal == 0, end, jnp.minimum(end, pos)) + row_seg[block] * DOC_STEP
        start = low * BLK + row_seg[block] * DOC_STEP
        wide = jnp.broadcast_to(own_line, (BLK, ROWS))
        inside.append(
            (wide >= jnp.concatenate([start, start], axis=1)) & (wide <= jnp.concatenate([end, end], axis=1))
        )
    hidden = jnp.where(jnp.concatenate(inside, axis=0), 0.0, MASKED)
    for part_at in range(GROUP):
        rows = slice(part_at * ROWS, (part_at + 1) * ROWS)
        turn_hidden = by_turn(hidden, part_at // 2)
        score = exact(scaled[rows, 0:HD], own_key)
        score = jnp.where(jnp.concatenate([turn_hidden, turn_hidden], axis=0) < 0.0, MASKED, score)
        new = jnp.broadcast_to(jnp.max(score, axis=1, keepdims=True), (ROWS, HD))
        top[rows, :] = new
        expo = jnp.concatenate(
            [jnp.exp2((score[:, at * BLK : (at + 1) * BLK] - new) * SCALE).astype(jnp.bfloat16) for at in range(2)],
            axis=1,
        )
        total[rows, :] = exact(expo, own_value)

    def attend(*work):
        ready = []
        for pieces, turns in work:
            key_parts, value_parts = [], []
            for role, index in pieces:
                blocks = []
                for block, line in enumerate(line_of(role, index)):
                    spot = jnp.broadcast_to(line, (CLASSES, BLK))
                    seen = (spot >= class_from) & (spot <= class_to)
                    extra = jnp.where(seen, 0.0, MASKED).astype(jnp.bfloat16)
                    blocks.append(
                        jnp.concatenate([held[role, index, block * BLK : (block + 1) * BLK, :], extra], axis=0)
                    )
                key_parts.append(jnp.concatenate(blocks, axis=1))
                value_parts.append(with_ones(held[role, index, KSEG:PIECE, :]))
            value_all = jnp.concatenate(value_parts, axis=0)
            for part_at in [2 * turn + half for turn in turns for half in range(2)]:
                rows = slice(part_at * ROWS, (part_at + 1) * ROWS)
                scores = []
                for key in key_parts:
                    score = exact(scaled[rows, 0 : HD + CLASSES], key)
                    scores += [score[:, 0:BLK], score[:, BLK : 2 * BLK]]
                ready.append((rows, scores, value_all))
        for rows, scores, value_all in ready:
            largest = functools.reduce(jnp.maximum, scores)
            old = top[rows, :]
            new = jnp.maximum(old, jnp.max(largest, axis=1, keepdims=True))
            top[rows, :] = new
            factor = jnp.exp2((old - new) * SCALE)
            expo = jnp.concatenate(
                [jnp.exp2((score - new) * SCALE).astype(jnp.bfloat16) for score in scores], axis=1
            )
            added = exact(expo, value_all)
            total[rows, 0:HD] = total[rows, 0:HD] * factor + added[:, 0:HD]
            total[rows, HD : 2 * HD] = total[rows, HD : 2 * HD] * factor + added[:, HD : 2 * HD]

    def block_core(at):
        return jnp.where((at % 16) // 8 == 0, core, other)

    came = iota((BLK, MIXED), 1)
    expand = one_hot(iota((BLK, MIXED), 0) == 2 * (2 * (came // 16) + block_core(came)) + core)
    owner_rows = jnp.broadcast_to(owner[...].astype(jnp.float32), (8, BLK)).astype(jnp.bfloat16)
    owner_of = exact(owner_rows, expand)[0:1, :].astype(jnp.int32)
    code_in = owner_of * 8 + iota((1, MIXED), 1) % 8
    leaves = iota((MIXED, BLK), 0)
    code_out = (2 * (leaves // 16) + block_core(leaves)) * 8 + leaves % 8
    for at in range(MIXED // BLK):
        columns = slice(at * BLK, (at + 1) * BLK)
        mix[:, columns] = one_hot(code_out == jnp.broadcast_to(code_in[:, columns], (MIXED, BLK)))

    at_out, at_in = iota((ROWS, ROWS), 0), iota((ROWS, ROWS), 1)
    shuffle[0] = one_hot(at_in == (at_out % 8) * TURN + at_out // 8)
    shuffle[1] = one_hot(at_in == (at_out % TURN) * 8 + ((at_out % 64) // TURN) * GROUP + at_out // 64)

    start = (2 * CHIPS - 1) % BATCH
    steps = (2 * CHIPS - 1) // BATCH
    reached = [min(CHIPS - 1, (start + BATCH * step) // 2 + LOOKAHEAD) for step in range(steps)] + [CHIPS - 1]

    def events(step, low, high):
        if high - low == 1:
            indices = tuple(range(reached[low] + 1, reached[low + 1] + 1))
            if indices:
                forward(indices)
            return
        middle = (low + high) // 2

        @pl.when(step < middle)
        def _():
            events(step, low, middle)

        @pl.when(step >= middle)
        def _():
            events(step, middle, high)

    def used(at):
        own = at % 2
        return (core + 1 + own) % 2, (at + own) // 2

    def batch(step, get):
        return [get(start + BATCH * step + each) for each in range(BATCH)]

    def take(step):
        last = 2 * step + 3

        @pl.when(step < steps - 1)
        def _():
            pair_copy(other, last).wait_recv()

        @pl.when(step == steps - 1)
        def _():
            copy((other, CHIPS - 1), "all", 0, CHIPS - 1, me).wait_recv()

        return batch(step, used)

    forward(tuple(range(1, reached[0] + 1)))
    copy((other, 0), "all", 0, 0, me).wait_recv()
    pair_copy(other, 1).wait_recv()
    attend(([used(jnp.int32(at)) for at in range(start)], (0, 1)))

    def both_halves(step, carry):
        events(step, 0, steps)
        attend((take(step), (0, 1)))
        return carry

    lax.fori_loop(0, steps, both_halves, 0)

    def swap(turn, way):
        return pltpu.make_async_remote_copy(
            src_ref=swap_out.at[way, turn], dst_ref=swap_in.at[way, turn],
            send_sem=swap_send.at[way, turn], recv_sem=swap_recv.at[way, turn],
            device_id=sibling, device_id_type=MESH,
        )

    def spread(turn, way):
        target = spread_in if way == 0 else back_in

        def one(step, carry):
            there = ctx_of((place.x + step // NZ) % NX, (place.z + step % NZ) % NZ, core)
            pltpu.make_async_remote_copy(
                src_ref=spread_out.at[way, turn, there // CORES], dst_ref=target.at[turn, place.chip_here],
                send_sem=spread_send.at[way, turn], recv_sem=spread_recv.at[way, turn],
                device_id=place.device(there), device_id_type=MESH,
            ).start()
            return carry

        lax.fori_loop(1, CHIPS, one, 0)
        target[turn, place.chip_here] = spread_out[way, turn, place.chip_here]

    def spread_arrived(turn, way):
        target = spread_in if way == 0 else back_in
        many = target.at[turn, pl.ds(0, CHIPS - 1)]
        pltpu.make_async_copy(many, many, spread_recv.at[way, turn]).wait()

    def spread_sent(turn, way):
        many = spread_out.at[way, turn, pl.ds(0, CHIPS - 1)]
        pltpu.make_async_copy(many, many, spread_send.at[way, turn]).wait()

    def attended(turn):
        return [
            (total[rows, 0:HD] / total[rows, HD : 2 * HD]).astype(jnp.bfloat16)
            for rows in (rows_of(turn, head) for head in range(GROUP))
        ]

    def close(turn):
        done = attended(turn)
        for block in range(2):
            starts = [block * 2 * TURN + side * TURN for side in range(2)]
            planes = [done[head][start : start + TURN, :] for start in starts for head in range(GROUP)]
            owned[turn, block] = exact(shuffle[0], jnp.concatenate(planes, axis=0)).astype(jnp.bfloat16)
        swap_out[0, turn] = owned[turn, other]
        swap(turn, 0).start()

    def eights(rows):
        return rows.astype(jnp.float32).reshape(CHIPS, 8, HD)

    def deal(turn):
        swap(turn, 0).wait_recv()
        both = jnp.concatenate([eights(owned[turn, core]), eights(swap_in[0, turn])], axis=1)
        spread_out[0, turn] = both.astype(jnp.bfloat16)
        spread(turn, 0)

    def reorder(turn):
        spread_arrived(turn, 0)
        came_rows = spread_in[turn].reshape(MIXED, HD)
        spread_out[1, turn] = exact(mix[...], came_rows).astype(jnp.bfloat16).reshape(CHIPS, 16, HD)
        spread(turn, 1)

    def collect(turn):
        spread_arrived(turn, 1)
        landed = back_in[turn].astype(jnp.float32)
        owned[turn, core] = landed[:, 0:8, :].reshape(ROWS, HD).astype(jnp.bfloat16)
        swap_out[1, turn] = landed[:, 8:16, :].reshape(ROWS, HD).astype(jnp.bfloat16)
        swap(turn, 1).start()

    def give(turn, message):
        way = 1 if message % 2 == 0 else -1
        side = (0, 1, 1, 0, 0, 1)[message]
        dest = place.plane(2 if message < 2 else way)
        if message < 2:
            target = first_in.at[turn, message]
        else:
            target = last_in.at[turn, message % 2, side]
        return pltpu.make_async_remote_copy(
            src_ref=part.at[turn, dest, side], dst_ref=target,
            send_sem=sum_send.at[turn, message], recv_sem=sum_recv.at[turn, message],
            device_id={"ctx": me, "head": place.plane(way)}, device_id_type=MESH,
        )

    def owned_rows(turn):
        swap(turn, 1).wait_recv()
        owned[turn, other] = swap_in[1, turn]
        lefts = []
        for block in range(2):
            sorted_rows = exact(shuffle[1], owned[turn, block]).astype(jnp.bfloat16)
            lefts.append(jnp.concatenate([sorted_rows[64 * head : 64 * (head + 1), :] for head in range(GROUP)], axis=1))
        return jnp.concatenate(lefts, axis=0)

    def project(turn, left):
        for side in range(2):
            for at in range(2):
                start = side * HALF + at * (HALF // 2)
                product = exact(left, proj[:, start : start + HALF // 2]).astype(jnp.bfloat16)
                for dest in range(HEADS):
                    part[turn, dest, side, :, at * (HALF // 2) : (at + 1) * (HALF // 2)] = product[
                        dest * TURN : (dest + 1) * TURN, :
                    ]
        for message in range(4):
            give(turn, message).start()
    def relay(turn):
        for message in (4, 5):
            way = 1 if message == 4 else -1
            side = message - 4
            give(turn, message - 4).wait_recv()
            dest = place.plane(way)
            merged = part[turn, dest, side].astype(jnp.float32) + first_in[turn, side].astype(jnp.float32)
            part[turn, dest, side] = merged.astype(jnp.bfloat16)
            give(turn, message).start()

    def finish(turn):
        for message in range(2, 6):
            give(turn, message).wait_recv()
        for side in range(2):
            summed = part[turn, place.head, side].astype(jnp.float32)
            for way in range(2):
                summed = summed + last_in[turn, way, side].astype(jnp.float32)
            summed = summed.astype(jnp.bfloat16)
            if turn == 0:
                out[0:TURN, side * HALF : (side + 1) * HALF] = summed
                continue
            for at in range(HALF // HD):
                tiles_out[0, side * (HALF // HD) + at] = summed[:, at * HD : (at + 1) * HD]

    def tile_spread(way):
        target = tiles_in.at[0] if way == 0 else tiles_back

        def one(step, carry):
            there = ctx_of((place.x + step // NZ) % NX, (place.z + step % NZ) % NZ, core)
            pltpu.make_async_remote_copy(
                src_ref=tiles_out.at[way, there // CORES], dst_ref=target.at[place.chip_here],
                send_sem=tiles_send.at[way], recv_sem=tiles_recv.at[way],
                device_id=place.device(there), device_id_type=MESH,
            ).start()
            return carry

        lax.fori_loop(1, CHIPS, one, 0)
        target[place.chip_here] = tiles_out[way, place.chip_here]

    def tiles_wait(sem):
        many = tiles_back.at[pl.ds(0, CHIPS - 1)]
        pltpu.make_async_copy(many, many, sem).wait()

    tile_swap = pltpu.make_async_remote_copy(
        src_ref=tiles_in.at[0], dst_ref=tiles_in.at[1], send_sem=tiles_send.at[2], recv_sem=tiles_recv.at[2],
        device_id=sibling, device_id_type=MESH,
    )

    def tile_homes():
        homes = []
        for chip in range(CHIPS):
            mine = (owner[...] == CORES * chip + core) & (lane % 2 == place.head // 2)
            home = jnp.clip(jnp.sum(jnp.where(mine, lane, 0)) // 2, 0, CTX - 1)
            homes.append(home)
        return homes

    def tiles_choose(homes):
        tile_swap.wait_recv()
        for chip, home in enumerate(homes):
            tiles_out[1, chip] = tiles_in[(home + core) % 2, home // 2]

    loads[6].wait()
    project(1, jnp.concatenate(attended(1), axis=1))
    close(0)
    deal(0)
    relay(1)
    reorder(0)
    finish(1)
    tile_spread(0)
    collect(0)
    project(0, owned_rows(0))
    relay(0)
    homes = tile_homes()
    tiles_wait(tiles_recv.at[0])
    tile_swap.start()
    tiles_choose(homes)
    tile_spread(1)
    for role in range(2):

        @pl.when(core == role)
        def _(role=role):
            for index in range(CHIPS):
                for each in sends(role, index):
                    each.wait_send()

    finish(0)
    tiles_wait(tiles_recv.at[1])
    for at in range(CHIPS):
        out[TURN : 2 * TURN, at * HD : (at + 1) * HD] = tiles_back[at]

    for way in range(2):
        swap(0, way).wait_send()
        spread_sent(0, way)
        tiles_wait(tiles_send.at[way])
    tile_swap.wait_send()
    for turn in range(2):
        for message in range(6):
            give(turn, message).wait_send()


def local(queries, keys, values, segments, block_ranges, owner, out_proj):
    anywhere = pl.BlockSpec(memory_space=pltpu.HBM)
    bf16, i32, f32 = jnp.bfloat16, jnp.int32, jnp.float32
    dma = pltpu.SemaphoreType.DMA
    return pl.pallas_call(
        kernel,
        out_shape=jax.ShapeDtypeStruct((ROWS // HEADS, WIDE), bf16),
        in_specs=[anywhere] * 7,
        out_specs=pl.BlockSpec(memory_space=pltpu.VMEM),
        scratch_shapes=[
            pltpu.VMEM((ROWS, GROUP * HD), bf16),
            pltpu.VMEM((ROWS, HD), bf16),
            pltpu.VMEM((2, BLK), i32),
            pltpu.VMEM((3, 2 * CTX), i32),
            pltpu.VMEM((1, 2 * CTX), i32),
            pltpu.VMEM((GROUP * HD, WIDE), bf16),
            dma((7,)),
            pltpu.VMEM((2, CHIPS, PIECE, HD), bf16),
            pltpu.VMEM((GROUP * ROWS, 2 * HD), bf16),
            pltpu.VMEM((GROUP * ROWS, 2 * HD), f32),
            pltpu.VMEM((GROUP * ROWS, HD), f32),
            dma((2, CHIPS, 2)),
            dma((CHIPS, 5)),
            pltpu.VMEM((2, ROWS, ROWS), bf16),
            pltpu.VMEM((2, 2, ROWS, HD), bf16),
            pltpu.VMEM((2, 2, ROWS, HD), bf16),
            pltpu.VMEM((2, 2, CHIPS, 16, HD), bf16),
            pltpu.VMEM((2, CHIPS, 16, HD), bf16),
            pltpu.VMEM((2, CHIPS, 16, HD), bf16),
            pltpu.VMEM((MIXED, MIXED), bf16),
            pltpu.VMEM((2, 2, ROWS, HD), bf16),
            dma((2, 2)),
            dma((2, 2)),
            dma((2, 2)),
            dma((2, 2)),
            pltpu.VMEM((2, HEADS, 2, TURN, HALF), bf16),
            pltpu.VMEM((2, 2, TURN, HALF), bf16),
            pltpu.VMEM((2, 2, 2, TURN, HALF), bf16),
            dma((2, 6)),
            dma((2, 6)),
            pltpu.VMEM((2, CHIPS, TURN, HD), bf16),
            pltpu.VMEM((2, CHIPS, TURN, HD), bf16),
            pltpu.VMEM((CHIPS, TURN, HD), bf16),
            dma((3,)),
            dma((3,)),
        ],
        compiler_params=pltpu.CompilerParams(
            collective_id=0, has_side_effects=True, vmem_limit_bytes=60 << 20
        ),
        cost_estimate=pl.CostEstimate(
            flops=4 * GROUP * ROWS * ROWS * CTX * HD,
            bytes_accessed=GROUP * HD * WIDE * 2,
            transcendentals=GROUP * ROWS * ROWS * CTX,
        ),
        name="attend_and_project",
    )(
        queries, keys, values, segments.reshape(2, BLK), block_ranges.T, owner.reshape(1, 2 * CTX), out_proj
    )


def solution(mesh):
    return jax.shard_map(
        local,
        mesh=mesh,
        in_specs=(
            P("ctx", "head"),
            P("ctx", "head"),
            P("ctx", "head"),
            P("ctx"),
            P(),
            P(),
            P("head", None),
        ),
        out_specs=P(("ctx", "head"), None),
        check_vma=False,
    )
```
